512 devices in a mesh: dp: 64 (over z, y), rep: 8 (over x, core).
Axes of the slice: x: 4, y: 8, z: 8, core: 2. Of those that a mesh axis runs over, the one named last changes fastest.
Arguments:
- grads: float32 [64, 64, 256, 256], P('dp', None, 'rep'), may hold values from -5 to 5
- left_root: float32 [64, 2, 256, 256], P('dp', None, 'rep'), may hold values from -0.375 to 0.375
- right_root: float32 [64, 2, 256, 256], P('dp'), may hold values from -0.375 to 0.375
- momentum: float32 [64, 2, 256, 256], P('dp', None, 'rep'), may hold values from -6 to 6
- block_owner: int32 [64], replicated, may hold values from 0 to 63, as said below
- owner_counts: int32 [64], P('dp'), may hold values from 0 to 2, as said below
Outputs:
- update: float32 [64, 256, 256], P('dp', 'rep')
- new_momentum: float32 [64, 2, 256, 256], P('dp', None, 'rep')
The draws below stay inside these ranges and needn't reach their ends.
Inputs may be any that keep to these rules, and one draw needn't show every extreme that they name: `block_owner`: no owner holds more than 2 blocks and some owner holds exactly 2. owner_counts[o] is the number of blocks b with block_owner[b] = o.
All inputs are finite; a program needn't handle non-finite values.
Results may differ from the reference program's by a relative error of at most 0.00007.
Values sent between devices are 32-bit elements; how exact they have to be, the bound alone decides.
No kernel may reach another device: no remote copies, remote signals or barrier semaphores. Data moves between devices by JAX's collectives and lax.ppermute only.
A program may use at most 64 MiB of HBM per device.

```python
import jax
import jax.numpy as jnp
from jax import lax

BS = 256
NB = 64
MOST = 2
N_DP = 64


def owner_slots(key):
    first = jax.random.randint(jax.random.fold_in(key, 1), (), 0, N_DP)
    others = jax.random.permutation(jax.random.fold_in(key, 2), (N_DP - 1) * MOST)
    others = jnp.where(others >= first * MOST, others + MOST, others)
    chosen = jnp.concatenate([first * MOST + jnp.arange(MOST), others[:NB - MOST]])
    chosen = jax.random.permutation(jax.random.fold_in(key, 3), chosen)
    return (chosen // MOST).astype(jnp.int32)


def draw_block_owner(key, part):
    owners = owner_slots(key)
    return owners.astype(jnp.int32)


def draw_owner_counts(key, part):
    owners = owner_slots(key)
    hits = (owners[:, None] == jnp.arange(N_DP)[None, :]).astype(jnp.int32)
    return jnp.sum(hits, axis=0).astype(jnp.int32)


def with_spikes(values, stream_key, source, target, blocks, factor):
    def block_of(dim):
        return (jnp.arange(values.shape[dim]) // (values.shape[dim] // blocks)).reshape((-1,) + (1,) * (values.ndim - 1 - dim))

    one_side = jax.random.permutation(stream_key, blocks)[block_of(target)]
    second = (block_of(target) + blocks // 2) % blocks
    return jnp.where((block_of(source) == one_side) | (block_of(source) == second), factor * values, values)


def shard_levels(own_key, extent, cuts, low, high):
    loudness = 1.0
    for axis_at, shards_of in cuts:
        steps = jax.random.uniform(jax.random.fold_in(jax.random.fold_in(own_key, 6), axis_at), (shards_of,), jnp.float32, low / len(cuts), high / len(cuts))
        loudness = loudness * jnp.repeat(jnp.exp(steps), extent[axis_at] // shards_of).reshape((-1,) + (1,) * (len(extent) - 1 - axis_at))
    return loudness


def centred(rng, shape, spread, limit, cuts=(), held_as=jnp.bfloat16):
    array = jax.random.normal(rng, shape, jnp.float32) * spread
    if len(cuts) > 0:
        array = shard_levels(rng, shape, cuts, -0.22, 0.18) * array
    return jnp.clip(array, min=-limit, max=limit).astype(held_as)


def noise_with(key, dims, width, reach, split, heavy, kind=jnp.bfloat16):
    values = width * jax.random.normal(key, dims, jnp.float32)
    if split:
        values = values * shard_levels(key, dims, split, -0.22, 0.18)
    return jnp.clip(with_spikes(values, jax.random.fold_in(key, 3), *heavy), -reach, reach).astype(kind)


def setup_inputs(seed: int = 0) -> dict:
    key_of = jax.random.split(jax.random.key(seed), 7)
    grads = noise_with(key_of[0], (N_DP, NB, BS, BS), 0.125, 5.0, ((0, 64), (2, 8)), (0, 1, 64, 4.0), jnp.float32)
    left_root = centred(key_of[1], (N_DP, MOST, BS, BS), BS ** -0.5, 0.375, ((0, 64), (2, 8)), jnp.float32)
    right_root = centred(key_of[2], (N_DP, MOST, BS, BS), BS ** -0.5, 0.375, ((0, 64),), jnp.float32)
    momentum = centred(key_of[3], (N_DP, MOST, BS, BS), 1.0, 6.0, ((0, 64), (2, 8)), jnp.float32)
    block_owner = draw_block_owner(jax.random.fold_in(key_of[6], 71), 0)
    owner_counts = draw_owner_counts(jax.random.fold_in(key_of[6], 71), 0)
    return {"grads": grads, "left_root": left_root, "right_root": right_root, "momentum": momentum, "block_owner": block_owner, "owner_counts": owner_counts}


BETA = 0.9
EPS = 1e-06

def reference(grads, left_root, right_root, momentum, block_owner, owner_counts):
    total = lax.optimization_barrier(jnp.sum(grads, axis=0))
    count = block_owner.shape[0]
    earlier = jnp.arange(count)[:, None] > jnp.arange(count)[None, :]
    same_owner = block_owner[:, None] == block_owner[None, :]
    slot_of = lax.optimization_barrier(jnp.sum((earlier & same_owner).astype(jnp.int32), axis=1)).astype(jnp.int32)
    entries = total.shape[1] * total.shape[2]

    def one_block(index):
        owner = block_owner[index]
        slot = slot_of[index]
        gradient = total[index]
        right_part = jnp.dot(gradient, right_root[owner, slot], precision=lax.Precision.HIGHEST, preferred_element_type=jnp.float32)
        precond = jnp.dot(left_root[owner, slot], right_part, precision=lax.Precision.HIGHEST, preferred_element_type=jnp.float32)
        graft = jnp.sqrt(jnp.sum(gradient * gradient) / entries) / jnp.sqrt(jnp.sum(precond * precond) / entries + EPS)
        direction = graft * precond
        fresh = BETA * momentum[owner, slot] + direction
        return (BETA * fresh + direction, direction)
    update, directions = lax.map(one_block, jnp.arange(count).astype(jnp.int32))
    used = jnp.arange(momentum.shape[1])[None, :] < owner_counts[:, None]
    base = jnp.where(used[:, :, None, None], BETA * momentum, momentum)
    new_momentum = base.at[block_owner, slot_of].add(directions)
    return (update, new_momentum)
```

```python
import jax
import jax.numpy as jnp
from jax import lax
from jax.sharding import Mesh, PartitionSpec as P

BETA = 0.9
EPS = 1e-06
AXES = ("z", "y", "x", "c")
HIGHEST = lax.Precision.HIGHEST


def device(z, y, x, c, sizes):
    return ((z * sizes[1] + y) * sizes[2] + x) * sizes[3] + c


def lines(sizes, along):
    groups = []
    for x in range(sizes[2]):
        for c in range(sizes[3]):
            for fixed in range(sizes[0]):
                if along[c] == "y":
                    groups.append([device(fixed, i, x, c, sizes) for i in range(sizes[1])])
                else:
                    groups.append([device(i, fixed, x, c, sizes) for i in range(sizes[0])])
    return groups


def make(sizes):
    side = sizes[0]
    reps = sizes[2] * sizes[3]
    first_lines = lines(sizes, ("y", "z"))
    second_lines = lines(sizes, ("z", "y"))

    def exchange(blocks, groups):
        return lax.all_to_all(blocks, AXES, 0, 0, tiled=True, axis_index_groups=groups)

    def on_device(grads, left_root, right_root, momentum, block_owner, owner_counts):
        parts = grads[0]
        nb, rows, order = parts.shape
        slots = left_root.shape[1]
        core = lax.axis_index("c")
        z, y = lax.axis_index("z"), lax.axis_index("y")
        flip = core == 1
        u = jnp.where(flip, z, y)
        w = jnp.where(flip, y, z)
        key = jnp.where(flip, (block_owner % side) * side + block_owner // side, block_owner)
        ids = jnp.arange(nb)
        less = key[None, :] < key[:, None]
        earlier = (key[None, :] == key[:, None]) & (ids[None, :] < ids[:, None])
        slot_of = jnp.sum(earlier.astype(jnp.int32), axis=1)
        rank = jnp.sum(less.astype(jnp.int32), axis=1) + slot_of
        hit = rank[None, :] == ids[:, None]
        block_at = jnp.sum(jnp.where(hit, ids[None, :], 0), axis=1)
        key_at = jnp.sum(jnp.where(hit, key[None, :], 0), axis=1)
        start = jnp.sum((key[None, :] < side * jnp.arange(side)[:, None]).astype(jnp.int32), axis=1)
        my_start = jnp.sum((key < w * side + u).astype(jnp.int32))
        first = (start - u + side - 1) // side

        send = jnp.take(parts, block_at.reshape(nb // side, side).T.reshape(nb), axis=0)
        got = exchange(send, first_lines)
        part = jnp.sum(got.reshape(side, nb // side, rows, order), axis=0)
        picks = jnp.clip(first[:, None] + jnp.arange(slots)[None, :], 0, nb // side - 1).reshape(-1)
        got = exchange(jnp.take(part, picks, axis=0), second_lines)
        held = jnp.sum(got.reshape(side, slots, rows, order), axis=0)
        at = jnp.clip(lax.dynamic_index_in_dim(first, w, 0, False) * side + u, 0, nb - 1)
        here = lax.dynamic_index_in_dim(key_at, at, 0, False) % side
        picks = (jnp.arange(side) != here).astype(jnp.int32)
        got = exchange(jnp.take(held, picks, axis=0), first_lines)
        gradient = jnp.take(got, (my_start + jnp.arange(slots)) % side, axis=0)

        lefts = lax.all_gather(left_root[0], ("x", "c"), axis=1, tiled=True)
        rights = right_root[0]
        whole = lax.all_gather(gradient, ("x", "c"), axis=1, tiled=True)
        right_part = jnp.einsum("sak,skc->sac", whole, rights, precision=HIGHEST)
        precond = jnp.einsum("sak,skc->sac", lefts, right_part, precision=HIGHEST)
        grad_square = jnp.sum(whole * whole, axis=(1, 2))
        pre_square = jnp.sum(precond * precond, axis=(1, 2))
        entries = order * order
        graft = jnp.sqrt(grad_square / entries) / jnp.sqrt(pre_square / entries + EPS)
        me = lax.axis_index(("x", "c"))
        direction = graft[:, None, None] * lax.dynamic_slice_in_dim(precond, me * rows, rows, 1)
        moment = momentum[0]
        fresh = BETA * moment + direction
        update_owned = BETA * fresh + direction
        used = jnp.arange(slots) < owner_counts[0]
        new_moment = jnp.where(used[:, None, None], fresh, moment)

        got = exchange(jnp.tile(update_owned, (side, 1, 1)), first_lines)
        others = jnp.where(flip, u * side + jnp.arange(side), jnp.arange(side) * side + u)
        picks = jnp.take((key % side) * slots + slot_of, others)
        got = exchange(jnp.take(got, picks, axis=0), second_lines)
        mine = z * side + y
        source = lax.dynamic_index_in_dim(key, mine, 0, False) // side
        update = lax.dynamic_index_in_dim(got, source, 0, True)
        return (update, new_moment[None])

    return on_device


def solution(mesh):
    sizes = (8, 8, 4, 2)
    fine = Mesh(mesh.devices.reshape(sizes), AXES)
    dp, rep = ("z", "y"), ("x", "c")
    in_specs = (
        P(dp, None, rep, None),
        P(dp, None, rep, None),
        P(dp, None, None, None),
        P(dp, None, rep, None),
        P(),
        P(dp),
    )
    out_specs = (P(dp, rep, None), P(dp, None, rep, None))
    return jax.shard_map(
        make(sizes), mesh=fine, in_specs=in_specs, out_specs=out_specs, check_vma=False
    )
```

```python
import jax
import jax.numpy as jnp
from jax import lax
from jax.sharding import Mesh, PartitionSpec as P

BETA = 0.9
EPS = 1e-06
AXES = ("z", "y", "x", "c")
HIGHEST = lax.Precision.HIGHEST


def device(z, y, x, c, sizes):
    return ((z * sizes[1] + y) * sizes[2] + x) * sizes[3] + c


def lines(sizes, along):
    groups = []
    for x in range(sizes[2]):
        for c in range(sizes[3]):
            for fixed in range(sizes[0]):
                if along[c] == "y":
                    groups.append([device(fixed, i, x, c, sizes) for i in range(sizes[1])])
                else:
                    groups.append([device(i, fixed, x, c, sizes) for i in range(sizes[0])])
    return groups


def make(sizes):
    side = sizes[0]
    reps = sizes[2] * sizes[3]
    first_lines = lines(sizes, ("y", "z"))
    second_lines = lines(sizes, ("z", "y"))

    rep_lines = [
        [device(z, y, x, c, sizes) for x in range(sizes[2]) for c in range(sizes[3])]
        for z in range(sizes[0])
        for y in range(sizes[1])
    ]

    def gather_any_order(rows):
        other = lax.ppermute(rows, "c", [(0, 1), (1, 0)])
        chip = jnp.concatenate([rows, other], axis=1)
        away = [
            lax.ppermute(chip, "x", [(i, (i + k) % sizes[2]) for i in range(sizes[2])])
            for k in range(1, sizes[2])
        ]
        return jnp.concatenate([chip, *away], axis=1)

    def exchange(blocks, groups):
        return lax.all_to_all(blocks, AXES, 0, 0, tiled=True, axis_index_groups=groups)

    def pick(blocks, index):
        return blocks.at[index].get(mode="promise_in_bounds")

    def on_device(grads, left_root, right_root, momentum, block_owner, owner_counts):
        parts = grads[0]
        nb, rows, order = parts.shape
        slots = left_root.shape[1]
        core = lax.axis_index("c")
        z, y = lax.axis_index("z"), lax.axis_index("y")
        flip = core == 1
        u = jnp.where(flip, z, y)
        w = jnp.where(flip, y, z)
        key = jnp.where(flip, (block_owner % side) * side + block_owner // side, block_owner)
        ids = jnp.arange(nb)
        less = key[None, :] < key[:, None]
        earlier = (key[None, :] == key[:, None]) & (ids[None, :] < ids[:, None])
        slot_of = jnp.sum(earlier.astype(jnp.int32), axis=1)
        rank = jnp.sum(less.astype(jnp.int32), axis=1) + slot_of
        hit = rank[None, :] == ids[:, None]
        block_at = jnp.sum(jnp.where(hit, ids[None, :], 0), axis=1)
        key_at = jnp.sum(jnp.where(hit, key[None, :], 0), axis=1)
        start = jnp.sum((key[None, :] < side * jnp.arange(side)[:, None]).astype(jnp.int32), axis=1)
        my_start = jnp.sum((key < w * side + u).astype(jnp.int32))
        first = (start - u + side - 1) // side

        send = pick(parts, block_at.reshape(nb // side, side).T.reshape(nb))
        got = exchange(send, first_lines)
        lefts = gather_any_order(left_root[0])
        got, lefts = lax.optimization_barrier((got, lefts))
        part = jnp.sum(got.reshape(side, nb // side, rows, order), axis=0)
        picks = jnp.clip(first[:, None] + jnp.arange(slots)[None, :], 0, nb // side - 1).reshape(-1)
        got = exchange(pick(part, picks), second_lines)
        held = jnp.sum(got.reshape(side, slots, rows, order), axis=0)
        at = jnp.clip(lax.dynamic_index_in_dim(first, w, 0, False) * side + u, 0, nb - 1)
        here = lax.dynamic_index_in_dim(key_at, at, 0, False) % side
        picks = (jnp.arange(side) != here).astype(jnp.int32)
        got = exchange(pick(held, picks), first_lines)
        gradient = pick(got, jnp.tile((my_start + jnp.arange(slots)) % side, reps))

        rights = right_root[0]
        got = exchange(gradient, rep_lines).reshape(reps, slots, rows, order)
        whole = got.transpose(1, 0, 2, 3).reshape(slots, order, order)
        right_part = jnp.einsum("sak,skc->sac", whole, rights, precision=HIGHEST)
        precond = jnp.einsum("sak,skc->sac", lefts, right_part, precision=HIGHEST)
        grad_square = jnp.sum(whole * whole, axis=(1, 2))
        pre_square = jnp.sum(precond * precond, axis=(1, 2))
        entries = order * order
        graft = jnp.sqrt(grad_square / entries) / jnp.sqrt(pre_square / entries + EPS)
        direction = graft[:, None, None] * precond[:, :rows]
        moment = momentum[0]
        fresh = BETA * moment + direction
        update_owned = BETA * fresh + direction
        used = jnp.arange(slots) < owner_counts[0]
        new_moment = jnp.where(used[:, None, None], fresh, moment)

        got = exchange(jnp.tile(update_owned, (side, 1, 1)), first_lines)
        others = jnp.where(flip, u * side + jnp.arange(side), jnp.arange(side) * side + u)
        picks = pick((key % side) * slots + slot_of, others)
        got = exchange(pick(got, picks), second_lines)
        mine = z * side + y
        source = lax.dynamic_index_in_dim(key, mine, 0, False) // side
        update = lax.dynamic_index_in_dim(got, source, 0, True)
        return (update, new_moment[None])

    return on_device


def solution(mesh):
    sizes = (8, 8, 4, 2)
    fine = Mesh(mesh.devices.reshape(sizes), AXES)
    dp, rep = ("z", "y"), ("x", "c")
    in_specs = (
        P(dp, None, rep, None),
        P(dp, None, rep, None),
        P(dp, None, None, None),
        P(dp, None, rep, None),
        P(),
        P(dp),
    )
    out_specs = (P(dp, rep, None), P(dp, None, rep, None))
    return jax.shard_map(
        make(sizes), mesh=fine, in_specs=in_specs, out_specs=out_specs, check_vma=False
    )
```

```python
import jax
import jax.numpy as jnp
from jax import lax
from jax.experimental import pallas as pl
from jax.experimental.pallas import tpu as pltpu
from jax.sharding import Mesh, PartitionSpec as P

BETA = 0.9
EPS = 1e-06
AXES = ("z", "y", "x", "c")
HIGHEST = lax.Precision.HIGHEST


def device(z, y, x, c, sizes):
    return ((z * sizes[1] + y) * sizes[2] + x) * sizes[3] + c


def lines(sizes, along):
    groups = []
    for x in range(sizes[2]):
        for c in range(sizes[3]):
            for fixed in range(sizes[0]):
                if along[c] == "y":
                    groups.append([device(fixed, i, x, c, sizes) for i in range(sizes[1])])
                else:
                    groups.append([device(i, fixed, x, c, sizes) for i in range(sizes[0])])
    return groups


VMEM = pl.BlockSpec(memory_space=pltpu.VMEM)
SMEM = pl.BlockSpec(memory_space=pltpu.SMEM)


def local_call(body, outs, ins, args):
    return pl.pallas_call(
        body,
        out_shape=outs,
        in_specs=ins,
        out_specs=jax.tree.map(lambda _: VMEM, outs),
        compiler_params=pltpu.CompilerParams(vmem_limit_bytes=24 * 2**20),
    )(*args)


def sum_and_pick(got, index, sources):
    each, count = got.shape[0] // sources, index.shape[0]

    def body(index_ref, got_ref, out_ref):
        for i in range(count):
            at = index_ref[i]
            total = got_ref[at]
            for s in range(1, sources):
                total = total + got_ref[s * each + at]
            out_ref[i] = total

    out = jax.ShapeDtypeStruct((count, *got.shape[1:]), got.dtype)
    return local_call(body, out, [SMEM, VMEM], (index, got))


def pick_and_repeat(got, index, times):
    count = index.shape[0]

    def body(index_ref, got_ref, out_ref):
        for i in range(count):
            block = got_ref[index_ref[i]]
            for t in range(times):
                out_ref[t * count + i] = block

    out = jax.ShapeDtypeStruct((times * count, *got.shape[1:]), got.dtype)
    return local_call(body, out, [SMEM, VMEM], (index, got))


def step(got, lefts, rights, moment, count, times):
    slots, rows, order = moment.shape
    reps = order // rows

    def body(count_ref, got_ref, left_ref, right_ref, moment_ref, moment_out_ref, send_ref):
        held = count_ref[0]
        for s in range(slots):
            whole = jnp.concatenate([got_ref[r * slots + s] for r in range(reps)], axis=0)
            right_part = jnp.dot(
                whole, right_ref[s], precision=HIGHEST, preferred_element_type=jnp.float32
            )
            precond = jnp.dot(
                left_ref[s], right_part, precision=HIGHEST, preferred_element_type=jnp.float32
            )
            entries = order * order
            grad_mean = jnp.sum(whole * whole, keepdims=True) / entries
            pre_mean = jnp.sum(precond * precond, keepdims=True) / entries
            graft = jnp.sqrt(grad_mean) / jnp.sqrt(pre_mean + EPS)
            direction = graft * precond[:rows]
            before = moment_ref[s]
            fresh = BETA * before + direction
            update = BETA * fresh + direction
            moment_out_ref[s] = jnp.where(s < held, fresh, before)
            for t in range(times):
                send_ref[t * slots + s] = update

    outs = (
        jax.ShapeDtypeStruct(moment.shape, moment.dtype),
        jax.ShapeDtypeStruct((times * slots, rows, order), moment.dtype),
    )
    return local_call(
        body, outs, [SMEM, VMEM, VMEM, VMEM, VMEM], (count, got, lefts, rights, moment)
    )


def make(sizes):
    side = sizes[0]
    reps = sizes[2] * sizes[3]
    first_lines = lines(sizes, ("y", "z"))
    second_lines = lines(sizes, ("z", "y"))

    rep_lines = [
        [device(z, y, x, c, sizes) for x in range(sizes[2]) for c in range(sizes[3])]
        for z in range(sizes[0])
        for y in range(sizes[1])
    ]

    def gather_any_order(rows):
        other = lax.ppermute(rows, "c", [(0, 1), (1, 0)])
        chip = jnp.concatenate([rows, other], axis=1)
        away = [
            lax.ppermute(chip, "x", [(i, (i + k) % sizes[2]) for i in range(sizes[2])])
            for k in range(1, sizes[2])
        ]
        return jnp.concatenate([chip, *away], axis=1)

    def exchange(blocks, groups):
        return lax.all_to_all(blocks, AXES, 0, 0, tiled=True, axis_index_groups=groups)

    def pick(blocks, index):
        return blocks.at[index].get(mode="promise_in_bounds")

    def on_device(grads, left_root, right_root, momentum, block_owner, owner_counts):
        parts = grads[0]
        nb, rows, order = parts.shape
        slots = left_root.shape[1]
        core = lax.axis_index("c")
        z, y = lax.axis_index("z"), lax.axis_index("y")
        flip = core == 1
        u = jnp.where(flip, z, y)
        w = jnp.where(flip, y, z)
        key = jnp.where(flip, (block_owner % side) * side + block_owner // side, block_owner)
        ids = jnp.arange(nb)
        less = key[None, :] < key[:, None]
        earlier = (key[None, :] == key[:, None]) & (ids[None, :] < ids[:, None])
        slot_of = jnp.sum(earlier.astype(jnp.int32), axis=1)
        rank = jnp.sum(less.astype(jnp.int32), axis=1) + slot_of
        hit = rank[None, :] == ids[:, None]
        block_at = jnp.sum(jnp.where(hit, ids[None, :], 0), axis=1)
        key_at = jnp.sum(jnp.where(hit, key[None, :], 0), axis=1)
        start = jnp.sum((key[None, :] < side * jnp.arange(side)[:, None]).astype(jnp.int32), axis=1)
        my_start = jnp.sum((key < w * side + u).astype(jnp.int32))
        first = (start - u + side - 1) // side

        picks_two = jnp.clip(first[:, None] + jnp.arange(slots)[None, :], 0, nb // side - 1)
        at = jnp.clip(lax.dynamic_index_in_dim(first, w, 0, False) * side + u, 0, nb - 1)
        here = lax.dynamic_index_in_dim(key_at, at, 0, False) % side
        picks_three = (jnp.arange(side) != here).astype(jnp.int32)
        picks_own = (my_start + jnp.arange(slots)) % side
        others = jnp.where(flip, u * side + jnp.arange(side), jnp.arange(side) * side + u)
        picks_back = pick((key % side) * slots + slot_of, others)
        source = lax.dynamic_index_in_dim(key, z * side + y, 0, False) // side
        tables = (picks_two.reshape(-1), picks_three, picks_own, picks_back, source)

        got = exchange(pick(parts, block_at.reshape(nb // side, side).T.reshape(nb)), first_lines)
        lefts = gather_any_order(left_root[0])
        got, lefts, tables = lax.optimization_barrier((got, lefts, tables))
        picks_two, picks_three, picks_own, picks_back, source = tables
        got = exchange(sum_and_pick(got, picks_two, side), second_lines)
        got = exchange(sum_and_pick(got, picks_three, side), first_lines)
        got = exchange(pick_and_repeat(got, picks_own, reps), rep_lines)
        new_moment, send = step(got, lefts, right_root[0], momentum[0], owner_counts, side)
        got = exchange(send, first_lines)
        got = exchange(pick_and_repeat(got, picks_back, 1), second_lines)
        update = lax.dynamic_index_in_dim(got, source, 0, True)
        return (update, new_moment[None])

    return on_device


def solution(mesh):
    sizes = (8, 8, 4, 2)
    fine = Mesh(mesh.devices.reshape(sizes), AXES)
    dp, rep = ("z", "y"), ("x", "c")
    in_specs = (
        P(dp, None, rep, None),
        P(dp, None, rep, None),
        P(dp, None, None, None),
        P(dp, None, rep, None),
        P(),
        P(dp),
    )
    out_specs = (P(dp, rep, None), P(dp, None, rep, None))
    return jax.shard_map(
        make(sizes), mesh=fine, in_specs=in_specs, out_specs=out_specs, check_vma=False
    )
```

```python
import jax
import jax.numpy as jnp
from jax import lax
from jax.experimental import pallas as pl
from jax.experimental.pallas import tpu as pltpu
from jax.sharding import Mesh, PartitionSpec as P

BETA = 0.9
EPS = 1e-06
AXES = ("z", "y", "x", "c")
HIGHEST = lax.Precision.HIGHEST


def device(z, y, x, c, sizes):
    return ((z * sizes[1] + y) * sizes[2] + x) * sizes[3] + c


def lines(sizes, along):
    groups = []
    for x in range(sizes[2]):
        for c in range(sizes[3]):
            for fixed in range(sizes[0]):
                if along[c] == "y":
                    groups.append([device(fixed, i, x, c, sizes) for i in range(sizes[1])])
                else:
                    groups.append([device(i, fixed, x, c, sizes) for i in range(sizes[0])])
    return groups


VMEM = pl.BlockSpec(memory_space=pltpu.VMEM)
SMEM = pl.BlockSpec(memory_space=pltpu.SMEM)


ANY = pl.BlockSpec(memory_space=pl.ANY)
TWO, THREE, OWN, BACK, SOURCE, COUNT, TABLE = 0, 16, 24, 26, 34, 35, 36


def local_call(body, outs, ins, args, out_specs=None, scratch=()):
    return pl.pallas_call(
        body,
        out_shape=outs,
        in_specs=ins,
        out_specs=jax.tree.map(lambda _: VMEM, outs) if out_specs is None else out_specs,
        scratch_shapes=scratch,
        compiler_params=pltpu.CompilerParams(vmem_limit_bytes=24 * 2**20),
    )(*args)


def key_of(owner, flip, side):
    turned = (owner & (side - 1)) * side + owner // side
    return jnp.where(flip, turned, owner)


def sort_blocks(place_ref, owner_ref, slot_ref, start_ref, side):
    nb = owner_ref.shape[0]
    flip = place_ref[2] == 1
    for k in range(side * side):
        start_ref[k] = 0
    for b in range(nb):
        key = key_of(owner_ref[b], flip, side)
        slot_ref[b] = start_ref[key]
        start_ref[key] = slot_ref[b] + 1
    total = jnp.int32(0)
    for k in range(side * side):
        held = start_ref[k]
        start_ref[k] = total
        total = total + held


def deal(parts, place, block_owner, side):
    nb = parts.shape[0]

    def body(place_ref, owner_ref, parts_ref, out_ref, slot_ref, start_ref, sem):
        flip = place_ref[2] == 1
        sort_blocks(place_ref, owner_ref, slot_ref, start_ref, side)
        for b in range(nb):
            rank = start_ref[key_of(owner_ref[b], flip, side)] + slot_ref[b]
            to = (rank & (side - 1)) * (nb // side) + rank // side
            pltpu.make_async_copy(parts_ref.at[b], out_ref.at[to], sem).start()
        pltpu.make_async_copy(parts_ref, out_ref, sem).wait()

    scratch = [pltpu.SMEM((nb,), jnp.int32), pltpu.SMEM((side * side,), jnp.int32), pltpu.SemaphoreType.DMA(())]
    out = jax.ShapeDtypeStruct(parts.shape, parts.dtype)
    return local_call(body, out, [SMEM, SMEM, ANY], (place, block_owner, parts), ANY, scratch)


def tables(place, block_owner, owner_counts, side, slots):
    nb = block_owner.shape[0]

    def body(place_ref, owner_ref, count_ref, out_ref, slot_ref, start_ref, key_at_ref):
        z, y, flip = place_ref[0], place_ref[1], place_ref[2] == 1
        u, w = jnp.where(flip, z, y), jnp.where(flip, y, z)
        sort_blocks(place_ref, owner_ref, slot_ref, start_ref, side)
        for b in range(nb):
            key = key_of(owner_ref[b], flip, side)
            key_at_ref[start_ref[key] + slot_ref[b]] = key

        def first(line):
            return jnp.maximum(start_ref[line * side] - u + side - 1, 0) // side

        for line in range(side):
            for s in range(slots):
                out_ref[TWO + line * slots + s] = jnp.minimum(first(line) + s, nb // side - 1)
        here = key_at_ref[jnp.minimum(first(w) * side + u, nb - 1)] & (side - 1)
        for i in range(side):
            out_ref[THREE + i] = jnp.where(here == i, 0, 1)
        for s in range(slots):
            out_ref[OWN + s] = (start_ref[w * side + u] + s) & (side - 1)
        for i in range(side):
            b = jnp.where(flip, u * side + i, i * side + u)
            key = key_of(owner_ref[b], flip, side)
            out_ref[BACK + i] = (key & (side - 1)) * slots + slot_ref[b]
        out_ref[SOURCE] = key_of(owner_ref[z * side + y], flip, side) // side
        out_ref[COUNT] = count_ref[0]

    scratch = [pltpu.SMEM((nb,), jnp.int32), pltpu.SMEM((side * side,), jnp.int32), pltpu.SMEM((nb,), jnp.int32)]
    out = jax.ShapeDtypeStruct((TABLE,), jnp.int32)
    return local_call(body, out, [SMEM, SMEM, SMEM], (place, block_owner, owner_counts), SMEM, scratch)


def sum_and_pick(got, table, base, count, sources):
    each = got.shape[0] // sources

    def body(table_ref, got_ref, out_ref, held_ref, total_ref, sems):
        def fetch(s):
            part = pl.ds(s * each, each)
            return pltpu.make_async_copy(got_ref.at[part], held_ref.at[part], sems.at[s])

        for s in range(sources):
            fetch(s).start()
        for s in range(sources):
            fetch(s).wait()
            for i in range(each):
                block = held_ref[s * each + i]
                total_ref[i] = block if s == 0 else total_ref[i] + block
        for i in range(count):
            out_ref[i] = total_ref[table_ref[base + i]]

    out = jax.ShapeDtypeStruct((count, *got.shape[1:]), got.dtype)
    scratch = [
        pltpu.VMEM(got.shape, got.dtype),
        pltpu.VMEM((each, *got.shape[1:]), got.dtype),
        pltpu.SemaphoreType.DMA((sources,)),
    ]
    return local_call(body, out, [SMEM, ANY], (table, got), None, scratch)


def sum_and_pick_here(got, table, base, count, sources):
    each = got.shape[0] // sources

    def body(table_ref, got_ref, out_ref):
        for i in range(count):
            at = table_ref[base + i]
            total = got_ref[at]
            for s in range(1, sources):
                total = total + got_ref[s * each + at]
            out_ref[i] = total

    out = jax.ShapeDtypeStruct((count, *got.shape[1:]), got.dtype)
    return local_call(body, out, [SMEM, VMEM], (table, got))


def pick_and_repeat(got, table, base, count, times):
    def body(table_ref, got_ref, out_ref):
        for i in range(count):
            block = got_ref[table_ref[base + i]]
            for t in range(times):
                out_ref[t * count + i] = block

    out = jax.ShapeDtypeStruct((times * count, *got.shape[1:]), got.dtype)
    return local_call(body, out, [SMEM, VMEM], (table, got))


def step(got, factors, moment, table, times):
    slots, rows, order = moment.shape
    reps = order // rows

    def body(table_ref, got_ref, factor_ref, moment_ref, moment_out_ref, send_ref):
        held = table_ref[COUNT]
        for s in range(slots):
            whole = jnp.concatenate([got_ref[r * slots + s] for r in range(reps)], axis=0)
            right_part = jnp.dot(
                whole, factor_ref[slots + s], precision=HIGHEST, preferred_element_type=jnp.float32
            )
            precond = jnp.dot(
                factor_ref[s], right_part, precision=HIGHEST, preferred_element_type=jnp.float32
            )
            entries = order * order
            grad_mean = jnp.sum(whole * whole, keepdims=True) / entries
            pre_mean = jnp.sum(precond * precond, keepdims=True) / entries
            graft = jnp.sqrt(grad_mean) / jnp.sqrt(pre_mean + EPS)
            direction = graft * precond[:rows]
            before = moment_ref[s]
            fresh = BETA * before + direction
            update = BETA * fresh + direction
            moment_out_ref[s] = jnp.where(s < held, fresh, before)
            for t in range(times):
                send_ref[t * slots + s] = update

    outs = (
        jax.ShapeDtypeStruct(moment.shape, moment.dtype),
        jax.ShapeDtypeStruct((times * slots, rows, order), moment.dtype),
    )
    return local_call(
        body, outs, [SMEM, VMEM, VMEM, VMEM], (table, got, factors, moment)
    )


def make(sizes):
    side = sizes[0]
    reps = sizes[2] * sizes[3]
    first_lines = lines(sizes, ("y", "z"))
    second_lines = lines(sizes, ("z", "y"))

    rep_lines = [
        [device(z, y, x, c, sizes) for x in range(sizes[2]) for c in range(sizes[3])]
        for z in range(sizes[0])
        for y in range(sizes[1])
    ]

    def gather_any_order(rows):
        other = lax.ppermute(rows, "c", [(0, 1), (1, 0)])
        chip = jnp.concatenate([rows, other], axis=1)
        away = [
            lax.ppermute(chip, "x", [(i, (i + k) % sizes[2]) for i in range(sizes[2])])
            for k in range(1, sizes[2])
        ]
        return jnp.concatenate([chip, *away], axis=1)

    def exchange(blocks, groups):
        return lax.all_to_all(blocks, AXES, 0, 0, tiled=True, axis_index_groups=groups)

    def on_device(grads, left_root, right_root, momentum, block_owner, owner_counts):
        slots = left_root.shape[1]
        place = jnp.stack([lax.axis_index(a) for a in ("z", "y", "c")]).astype(jnp.int32)
        got = exchange(deal(grads[0], place, block_owner, side), first_lines)
        table = tables(place, block_owner, owner_counts, side, slots)
        factors = jnp.concatenate([gather_any_order(left_root[0]), right_root[0]], axis=0)
        got, factors, table = lax.optimization_barrier((got, factors, table))
        got = exchange(sum_and_pick(got, table, TWO, side * slots, side), second_lines)
        got = exchange(sum_and_pick_here(got, table, THREE, side, side), first_lines)
        got = exchange(pick_and_repeat(got, table, OWN, slots, reps), rep_lines)
        new_moment, send = step(got, factors, momentum[0], table, side)
        got = exchange(send, first_lines)
        got = exchange(pick_and_repeat(got, table, BACK, side, 1), second_lines)
        update = pick_and_repeat(got, table, SOURCE, 1, 1)
        return (update, new_moment[None])

    return on_device


def solution(mesh):
    sizes = (8, 8, 4, 2)
    fine = Mesh(mesh.devices.reshape(sizes), AXES)
    dp, rep = ("z", "y"), ("x", "c")
    in_specs = (
        P(dp, None, rep, None),
        P(dp, None, rep, None),
        P(dp, None, None, None),
        P(dp, None, rep, None),
        P(),
        P(dp),
    )
    out_specs = (P(dp, rep, None), P(dp, None, rep, None))
    return jax.shard_map(
        make(sizes), mesh=fine, in_specs=in_specs, out_specs=out_specs, check_vma=False
    )
```

```python
import jax
import jax.numpy as jnp
from jax import lax
from jax.experimental import pallas as pl
from jax.experimental.pallas import tpu as pltpu
from jax.sharding import Mesh, PartitionSpec as P

BETA = 0.9
EPS = 1e-06
AXES = ("z", "y", "x", "c")


def device(z, y, x, c, sizes):
    return ((z * sizes[1] + y) * sizes[2] + x) * sizes[3] + c


def lines(sizes, along):
    groups = []
    for x in range(sizes[2]):
        for c in range(sizes[3]):
            for fixed in range(sizes[0]):
                if along[c] == "y":
                    groups.append([device(fixed, i, x, c, sizes) for i in range(sizes[1])])
                else:
                    groups.append([device(i, fixed, x, c, sizes) for i in range(sizes[0])])
    return groups


VMEM = pl.BlockSpec(memory_space=pltpu.VMEM)
SMEM = pl.BlockSpec(memory_space=pltpu.SMEM)


ANY = pl.BlockSpec(memory_space=pl.ANY)
TWO, THREE, OWN, BACK, SOURCE, COUNT, CORE, TABLE = 0, 16, 24, 26, 34, 35, 36, 37


def local_call(body, outs, ins, args, out_specs=None, scratch=(), limit=24):
    return pl.pallas_call(
        body,
        out_shape=outs,
        in_specs=ins,
        out_specs=jax.tree.map(lambda _: VMEM, outs) if out_specs is None else out_specs,
        scratch_shapes=scratch,
        compiler_params=pltpu.CompilerParams(vmem_limit_bytes=limit * 2**20),
    )(*args)


def key_of(owner, flip, side):
    turned = (owner & (side - 1)) * side + owner // side
    return jnp.where(flip, turned, owner)


def sort_blocks(place_ref, owner_ref, slot_ref, start_ref, side):
    nb = owner_ref.shape[0]
    flip = place_ref[2] == 1
    for k in range(side * side):
        start_ref[k] = 0
    for b in range(nb):
        key = key_of(owner_ref[b], flip, side)
        slot_ref[b] = start_ref[key]
        start_ref[key] = slot_ref[b] + 1
    total = jnp.int32(0)
    for k in range(side * side):
        held = start_ref[k]
        start_ref[k] = total
        total = total + held


def deal(parts, place, block_owner, side):
    nb = parts.shape[0]

    def body(place_ref, owner_ref, parts_ref, out_ref, slot_ref, start_ref, sem):
        flip = place_ref[2] == 1
        sort_blocks(place_ref, owner_ref, slot_ref, start_ref, side)
        for b in range(nb):
            rank = start_ref[key_of(owner_ref[b], flip, side)] + slot_ref[b]
            to = (rank & (side - 1)) * (nb // side) + rank // side
            pltpu.make_async_copy(parts_ref.at[b], out_ref.at[to], sem).start()
        pltpu.make_async_copy(parts_ref, out_ref, sem).wait()

    scratch = [pltpu.SMEM((nb,), jnp.int32), pltpu.SMEM((side * side,), jnp.int32), pltpu.SemaphoreType.DMA(())]
    out = jax.ShapeDtypeStruct(parts.shape, parts.dtype)
    return local_call(body, out, [SMEM, SMEM, ANY], (place, block_owner, parts), ANY, scratch, 60)


def tables(place, block_owner, owner_counts, side, slots):
    nb = block_owner.shape[0]

    def body(place_ref, owner_ref, count_ref, out_ref, slot_ref, start_ref, key_at_ref):
        z, y, flip = place_ref[0], place_ref[1], place_ref[2] == 1
        u, w = jnp.where(flip, z, y), jnp.where(flip, y, z)
        sort_blocks(place_ref, owner_ref, slot_ref, start_ref, side)
        for b in range(nb):
            key = key_of(owner_ref[b], flip, side)
            key_at_ref[start_ref[key] + slot_ref[b]] = key

        def first(line):
            return jnp.maximum(start_ref[line * side] - u + side - 1, 0) // side

        for line in range(side):
            for s in range(slots):
                out_ref[TWO + line * slots + s] = jnp.minimum(first(line) + s, nb // side - 1)
        here = key_at_ref[jnp.minimum(first(w) * side + u, nb - 1)] & (side - 1)
        for i in range(side):
            out_ref[THREE + i] = jnp.where(here == i, 0, 1)
        for s in range(slots):
            out_ref[OWN + s] = (start_ref[w * side + u] + s) & (side - 1)
        for i in range(side):
            b = jnp.where(flip, u * side + i, i * side + u)
            key = key_of(owner_ref[b], flip, side)
            out_ref[BACK + i] = (key & (side - 1)) * slots + slot_ref[b]
        out_ref[SOURCE] = key_of(owner_ref[z * side + y], flip, side) // side
        out_ref[COUNT] = count_ref[0]
        out_ref[CORE] = place_ref[2]

    scratch = [pltpu.SMEM((nb,), jnp.int32), pltpu.SMEM((side * side,), jnp.int32), pltpu.SMEM((nb,), jnp.int32)]
    out = jax.ShapeDtypeStruct((TABLE,), jnp.int32)
    return local_call(body, out, [SMEM, SMEM, SMEM], (place, block_owner, owner_counts), SMEM, scratch)


def sum_and_pick(got, table, base, count, sources):
    each = got.shape[0] // sources

    def body(table_ref, got_ref, out_ref, held_ref, total_ref, sems):
        def fetch(s):
            part = pl.ds(s * each, each)
            return pltpu.make_async_copy(got_ref.at[part], held_ref.at[part], sems.at[s])

        for s in range(sources):
            fetch(s).start()
        for s in range(sources):
            fetch(s).wait()
            for i in range(each):
                block = held_ref[s * each + i]
                total_ref[i] = block if s == 0 else total_ref[i] + block
        for i in range(count):
            out_ref[i] = total_ref[table_ref[base + i]]

    out = jax.ShapeDtypeStruct((count, *got.shape[1:]), got.dtype)
    scratch = [
        pltpu.VMEM(got.shape, got.dtype),
        pltpu.VMEM((each, *got.shape[1:]), got.dtype),
        pltpu.SemaphoreType.DMA((sources,)),
    ]
    return local_call(body, out, [SMEM, ANY], (table, got), None, scratch)


def sum_and_pick_here(got, table, base, count, sources):
    each = got.shape[0] // sources

    def body(table_ref, got_ref, out_ref):
        for i in range(count):
            at = table_ref[base + i]
            total = got_ref[at]
            for s in range(1, sources):
                total = total + got_ref[s * each + at]
            out_ref[i] = total

    out = jax.ShapeDtypeStruct((count, *got.shape[1:]), got.dtype)
    return local_call(body, out, [SMEM, VMEM], (table, got))


def pick_and_repeat(got, table, base, count, times):
    def body(table_ref, got_ref, out_ref):
        for i in range(count):
            block = got_ref[table_ref[base + i]]
            for t in range(times):
                out_ref[t * count + i] = block

    out = jax.ShapeDtypeStruct((times * count, *got.shape[1:]), got.dtype)
    return local_call(body, out, [SMEM, VMEM], (table, got))


def halves(a):
    high = a.astype(jnp.bfloat16)
    return high, (a - high.astype(jnp.float32)).astype(jnp.bfloat16)


def product(a, b):
    (ah, al), (bh, bl) = halves(a), halves(b)

    def dot(p, q):
        return jnp.dot(p, q, preferred_element_type=jnp.float32)

    return dot(ah, bh) + (dot(ah, bl) + dot(al, bh))


def step(own, other, factors, moment, table, times):
    slots, rows, order = moment.shape
    chips = own.shape[0] // slots

    def body(table_ref, own_ref, other_ref, factor_ref, moment_ref, moment_out_ref, send_ref, whole_ref):
        held, core = table_ref[COUNT], table_ref[CORE]
        for s in range(slots):
            for x in range(chips):
                whole_ref[s, 2 * x + core] = own_ref[x * slots + s]
                whole_ref[s, 2 * x + 1 - core] = other_ref[x * slots + s]
        for s in range(slots):
            whole = whole_ref[s].reshape(order, order)
            right_part = product(whole, factor_ref[slots + s])
            precond = product(factor_ref[s], right_part)
            entries = order * order
            grad_mean = jnp.sum(whole * whole, keepdims=True) / entries
            pre_mean = jnp.sum(precond * precond, keepdims=True) / entries
            graft = jnp.sqrt(grad_mean) / jnp.sqrt(pre_mean + EPS)
            direction = graft * precond[:rows]
            before = moment_ref[s]
            fresh = BETA * before + direction
            update = BETA * fresh + direction
            moment_out_ref[s] = jnp.where(s < held, fresh, before)
            for t in range(times):
                send_ref[t * slots + s] = update

    outs = (
        jax.ShapeDtypeStruct(moment.shape, moment.dtype),
        jax.ShapeDtypeStruct((times * slots, rows, order), moment.dtype),
    )
    scratch = [pltpu.VMEM((slots, order // rows, rows, order), moment.dtype)]
    return local_call(
        body, outs, [SMEM, VMEM, VMEM, VMEM, VMEM], (table, own, other, factors, moment), None, scratch
    )


def make(sizes):
    side = sizes[0]
    first_lines = lines(sizes, ("y", "z"))
    second_lines = lines(sizes, ("z", "y"))

    chip_lines = [
        [device(z, y, x, c, sizes) for x in range(sizes[2])]
        for z in range(sizes[0])
        for y in range(sizes[1])
        for c in range(sizes[3])
    ]

    def gather_any_order(rows):
        other = lax.ppermute(rows, "c", [(0, 1), (1, 0)])
        chip = jnp.concatenate([rows, other], axis=1)
        away = [
            lax.ppermute(chip, "x", [(i, (i + k) % sizes[2]) for i in range(sizes[2])])
            for k in range(1, sizes[2])
        ]
        return jnp.concatenate([chip, *away], axis=1)

    def exchange(blocks, groups):
        return lax.all_to_all(blocks, AXES, 0, 0, tiled=True, axis_index_groups=groups)

    def on_device(grads, left_root, right_root, momentum, block_owner, owner_counts):
        slots = left_root.shape[1]
        place = jnp.stack([lax.axis_index(a) for a in ("z", "y", "c")]).astype(jnp.int32)
        got = exchange(deal(grads[0], place, block_owner, side), first_lines)
        table = tables(place, block_owner, owner_counts, side, slots)
        factors = jnp.concatenate([gather_any_order(left_root[0]), right_root[0]], axis=0)
        source = table[SOURCE].astype(jnp.uint32)
        got, factors, table, source = lax.optimization_barrier((got, factors, table, source))
        got = exchange(sum_and_pick(got, table, TWO, side * slots, side), second_lines)
        got = exchange(sum_and_pick_here(got, table, THREE, side, side), first_lines)
        own = exchange(pick_and_repeat(got, table, OWN, slots, sizes[2]), chip_lines)
        other = lax.ppermute(own, "c", [(0, 1), (1, 0)])
        new_moment, send = step(own, other, factors, momentum[0], table, side)
        got = exchange(send, first_lines)
        got = exchange(pick_and_repeat(got, table, BACK, side, 1), second_lines)
        zero = jnp.uint32(0)
        update = lax.dynamic_slice(got, (source, zero, zero), (1, *got.shape[1:]))
        return (update, new_moment[None])

    return on_device


def solution(mesh):
    sizes = (8, 8, 4, 2)
    fine = Mesh(mesh.devices.reshape(sizes), AXES)
    dp, rep = ("z", "y"), ("x", "c")
    in_specs = (
        P(dp, None, rep, None),
        P(dp, None, rep, None),
        P(dp, None, None, None),
        P(dp, None, rep, None),
        P(),
        P(dp),
    )
    out_specs = (P(dp, rep, None), P(dp, None, rep, None))
    return jax.shard_map(
        make(sizes), mesh=fine, in_specs=in_specs, out_specs=out_specs, check_vma=False
    )
```

```python
import jax
import jax.numpy as jnp
from jax import lax
from jax.experimental import pallas as pl
from jax.experimental.pallas import tpu as pltpu
from jax.sharding import Mesh, PartitionSpec as P

BETA = 0.9
EPS = 1e-06
AXES = ("z", "y", "x", "c")


def device(z, y, x, c, sizes):
    return ((z * sizes[1] + y) * sizes[2] + x) * sizes[3] + c


def lines(sizes, along):
    groups = []
    for x in range(sizes[2]):
        for c in range(sizes[3]):
            for fixed in range(sizes[0]):
                if along[c] == "y":
                    groups.append([device(fixed, i, x, c, sizes) for i in range(sizes[1])])
                else:
                    groups.append([device(i, fixed, x, c, sizes) for i in range(sizes[0])])
    return groups


VMEM = pl.BlockSpec(memory_space=pltpu.VMEM)
SMEM = pl.BlockSpec(memory_space=pltpu.SMEM)


ANY = pl.BlockSpec(memory_space=pl.ANY)
TWO, THREE, OWN, BACK, SOURCE, COUNT, CORE, TABLE = 0, 16, 24, 26, 34, 35, 36, 37


def local_call(body, outs, ins, args, out_specs=None, scratch=(), limit=24):
    return pl.pallas_call(
        body,
        out_shape=outs,
        in_specs=ins,
        out_specs=jax.tree.map(lambda _: VMEM, outs) if out_specs is None else out_specs,
        scratch_shapes=scratch,
        compiler_params=pltpu.CompilerParams(vmem_limit_bytes=limit * 2**20),
    )(*args)


def key_of(owner, flip, side):
    turned = (owner & (side - 1)) * side + owner // side
    return jnp.where(flip, turned, owner)


def sort_blocks(flip, owner_ref, slot_ref, start_ref, side):
    nb = owner_ref.shape[0]
    for k in range(side * side):
        start_ref[k] = 0
    for b in range(nb):
        key = key_of(owner_ref[b], flip, side)
        slot_ref[b] = start_ref[key]
        start_ref[key] = slot_ref[b] + 1
    total = jnp.int32(0)
    for k in range(side * side):
        held = start_ref[k]
        start_ref[k] = total
        total = total + held


def deal(parts, block_owner, side):
    nb = parts.shape[0]

    def body(owner_ref, parts_ref, out_ref, held_ref, slot_ref, start_ref, in_sem, out_sem):
        fetch = pltpu.make_async_copy(parts_ref, held_ref, in_sem)
        fetch.start()
        flip = lax.axis_index("c") == 1
        sort_blocks(flip, owner_ref, slot_ref, start_ref, side)
        fetch.wait()
        for b in range(nb):
            rank = start_ref[key_of(owner_ref[b], flip, side)] + slot_ref[b]
            to = (rank & (side - 1)) * (nb // side) + rank // side
            pltpu.make_async_copy(held_ref.at[b], out_ref.at[to], out_sem).start()
        pltpu.make_async_copy(held_ref, out_ref, out_sem).wait()

    scratch = [
        pltpu.VMEM(parts.shape, parts.dtype),
        pltpu.SMEM((nb,), jnp.int32),
        pltpu.SMEM((side * side,), jnp.int32),
        pltpu.SemaphoreType.DMA(()),
        pltpu.SemaphoreType.DMA(()),
    ]
    out = jax.ShapeDtypeStruct(parts.shape, parts.dtype)
    return local_call(body, out, [SMEM, ANY], (block_owner, parts), ANY, scratch, 60)


def tables(block_owner, owner_counts, side, slots):
    nb = block_owner.shape[0]

    def body(owner_ref, count_ref, out_ref, slot_ref, start_ref, key_at_ref):
        z, y, core = lax.axis_index("z"), lax.axis_index("y"), lax.axis_index("c")
        flip = core == 1
        u, w = jnp.where(flip, z, y), jnp.where(flip, y, z)
        sort_blocks(flip, owner_ref, slot_ref, start_ref, side)
        for b in range(nb):
            key = key_of(owner_ref[b], flip, side)
            key_at_ref[start_ref[key] + slot_ref[b]] = key

        def first(line):
            return jnp.maximum(start_ref[line * side] - u + side - 1, 0) // side

        for line in range(side):
            for s in range(slots):
                out_ref[TWO + line * slots + s] = jnp.minimum(first(line) + s, nb // side - 1)
        here = key_at_ref[jnp.minimum(first(w) * side + u, nb - 1)] & (side - 1)
        for i in range(side):
            out_ref[THREE + i] = jnp.where(here == i, 0, 1)
        for s in range(slots):
            out_ref[OWN + s] = (start_ref[w * side + u] + s) & (side - 1)
        for i in range(side):
            b = jnp.where(flip, u * side + i, i * side + u)
            key = key_of(owner_ref[b], flip, side)
            out_ref[BACK + i] = (key & (side - 1)) * slots + slot_ref[b]
        out_ref[SOURCE] = key_of(owner_ref[z * side + y], flip, side) // side
        out_ref[COUNT] = count_ref[0]
        out_ref[CORE] = core

    scratch = [pltpu.SMEM((nb,), jnp.int32), pltpu.SMEM((side * side,), jnp.int32), pltpu.SMEM((nb,), jnp.int32)]
    out = jax.ShapeDtypeStruct((TABLE,), jnp.int32)
    return local_call(body, out, [SMEM, SMEM], (block_owner, owner_counts), SMEM, scratch)


def sum_and_pick(got, table, base, count, sources):
    each = got.shape[0] // sources

    def body(table_ref, got_ref, out_ref, held_ref, total_ref, sems):
        def fetch(s):
            part = pl.ds(s * each, each)
            return pltpu.make_async_copy(got_ref.at[part], held_ref.at[part], sems.at[s])

        for s in range(sources):
            fetch(s).start()
        for s in range(sources):
            fetch(s).wait()
            for i in range(each):
                block = held_ref[s * each + i]
                total_ref[i] = block if s == 0 else total_ref[i] + block
        for i in range(count):
            out_ref[i] = total_ref[table_ref[base + i]]

    out = jax.ShapeDtypeStruct((count, *got.shape[1:]), got.dtype)
    scratch = [
        pltpu.VMEM(got.shape, got.dtype),
        pltpu.VMEM((each, *got.shape[1:]), got.dtype),
        pltpu.SemaphoreType.DMA((sources,)),
    ]
    return local_call(body, out, [SMEM, ANY], (table, got), None, scratch)


def sum_and_pick_here(got, table, base, count, sources):
    each = got.shape[0] // sources

    def body(table_ref, got_ref, out_ref):
        for i in range(count):
            at = table_ref[base + i]
            total = got_ref[at]
            for s in range(1, sources):
                total = total + got_ref[s * each + at]
            out_ref[i] = total

    out = jax.ShapeDtypeStruct((count, *got.shape[1:]), got.dtype)
    return local_call(body, out, [SMEM, VMEM], (table, got))


def pick_and_repeat(got, table, base, count, times):
    def body(table_ref, got_ref, out_ref):
        for i in range(count):
            block = got_ref[table_ref[base + i]]
            for t in range(times):
                out_ref[t * count + i] = block

    out = jax.ShapeDtypeStruct((times * count, *got.shape[1:]), got.dtype)
    return local_call(body, out, [SMEM, VMEM], (table, got))


def halves(a):
    high = a.astype(jnp.bfloat16)
    return high, (a - high.astype(jnp.float32)).astype(jnp.bfloat16)


def product(a, b):
    (ah, al), (bh, bl) = halves(a), halves(b)

    def dot(p, q):
        return jnp.dot(p, q, preferred_element_type=jnp.float32)

    return dot(ah, bh) + (dot(ah, bl) + dot(al, bh))


def step(own, other, factors, moment, table, times):
    slots, rows, order = moment.shape
    chips = own.shape[0] // slots

    def body(table_ref, own_ref, other_ref, factor_ref, moment_ref, moment_out_ref, send_ref, whole_ref):
        held, core = table_ref[COUNT], table_ref[CORE]
        for s in range(slots):
            for x in range(chips):
                whole_ref[s, 2 * x + core] = own_ref[x * slots + s]
                whole_ref[s, 2 * x + 1 - core] = other_ref[x * slots + s]
        for s in range(slots):
            whole = whole_ref[s].reshape(order, order)
            right_part = product(whole, factor_ref[slots + s])
            precond = product(factor_ref[s], right_part)
            entries = order * order
            grad_mean = jnp.sum(whole * whole, keepdims=True) / entries
            pre_mean = jnp.sum(precond * precond, keepdims=True) / entries
            graft = jnp.sqrt(grad_mean) / jnp.sqrt(pre_mean + EPS)
            direction = graft * precond[:rows]
            before = moment_ref[s]
            fresh = BETA * before + direction
            update = BETA * fresh + direction
            moment_out_ref[s] = jnp.where(s < held, fresh, before)
            for t in range(times):
                send_ref[t * slots + s] = update

    outs = (
        jax.ShapeDtypeStruct(moment.shape, moment.dtype),
        jax.ShapeDtypeStruct((times * slots, rows, order), moment.dtype),
    )
    scratch = [pltpu.VMEM((slots, order // rows, rows, order), moment.dtype)]
    return local_call(
        body, outs, [SMEM, VMEM, VMEM, VMEM, VMEM], (table, own, other, factors, moment), None, scratch
    )


def make(sizes):
    side = sizes[0]
    first_lines = lines(sizes, ("y", "z"))
    second_lines = lines(sizes, ("z", "y"))

    chip_lines = [
        [device(z, y, x, c, sizes) for x in range(sizes[2])]
        for z in range(sizes[0])
        for y in range(sizes[1])
        for c in range(sizes[3])
    ]

    def gather_any_order(rows):
        other = lax.ppermute(rows, "c", [(0, 1), (1, 0)])
        chip = jnp.concatenate([rows, other], axis=1)
        away = [
            lax.ppermute(chip, "x", [(i, (i + k) % sizes[2]) for i in range(sizes[2])])
            for k in range(1, sizes[2])
        ]
        return jnp.concatenate([chip, *away], axis=1)

    def exchange(blocks, groups):
        return lax.all_to_all(blocks, AXES, 0, 0, tiled=True, axis_index_groups=groups)

    def on_device(grads, left_root, right_root, momentum, block_owner, owner_counts):
        slots = left_root.shape[1]
        got = exchange(deal(grads[0], block_owner, side), first_lines)
        table = tables(block_owner, owner_counts, side, slots)
        factors = jnp.concatenate([gather_any_order(left_root[0]), right_root[0]], axis=0)
        source = table[SOURCE].astype(jnp.uint32)
        got, factors, table, source = lax.optimization_barrier((got, factors, table, source))
        got = exchange(sum_and_pick(got, table, TWO, side * slots, side), second_lines)
        got = exchange(sum_and_pick_here(got, table, THREE, side, side), first_lines)
        own = exchange(pick_and_repeat(got, table, OWN, slots, sizes[2]), chip_lines)
        other = lax.ppermute(own, "c", [(0, 1), (1, 0)])
        new_moment, send = step(own, other, factors, momentum[0], table, side)
        got = exchange(send, first_lines)
        got = exchange(pick_and_repeat(got, table, BACK, side, 1), second_lines)
        zero = jnp.uint32(0)
        update = lax.dynamic_slice(got, (source, zero, zero), (1, *got.shape[1:]))
        return (update, new_moment[None])

    return on_device


def solution(mesh):
    sizes = (8, 8, 4, 2)
    fine = Mesh(mesh.devices.reshape(sizes), AXES)
    dp, rep = ("z", "y"), ("x", "c")
    in_specs = (
        P(dp, None, rep, None),
        P(dp, None, rep, None),
        P(dp, None, None, None),
        P(dp, None, rep, None),
        P(),
        P(dp),
    )
    out_specs = (P(dp, rep, None), P(dp, None, rep, None))
    return jax.shard_map(
        make(sizes), mesh=fine, in_specs=in_specs, out_specs=out_specs, check_vma=False
    )
```

```python
import jax
import jax.numpy as jnp
from jax import lax
from jax.experimental import pallas as pl
from jax.experimental.pallas import tpu as pltpu
from jax.sharding import Mesh, PartitionSpec as P

BETA = 0.9
EPS = 1e-06
AXES = ("z", "y", "x", "c")


def device(z, y, x, c, sizes):
    return ((z * sizes[1] + y) * sizes[2] + x) * sizes[3] + c


def lines(sizes, along):
    groups = []
    for x in range(sizes[2]):
        for c in range(sizes[3]):
            for fixed in range(sizes[0]):
                if along[c] == "y":
                    groups.append([device(fixed, i, x, c, sizes) for i in range(sizes[1])])
                else:
                    groups.append([device(i, fixed, x, c, sizes) for i in range(sizes[0])])
    return groups


VMEM = pl.BlockSpec(memory_space=pltpu.VMEM)
SMEM = pl.BlockSpec(memory_space=pltpu.SMEM)


ANY = pl.BlockSpec(memory_space=pl.ANY)
TWO, THREE, OWN, BACK, COUNT, ROWS, SOURCE, TABLE = 0, 16, 24, 26, 34, 35, 36, 37


def local_call(body, outs, ins, args, out_specs=None, scratch=(), limit=24):
    return pl.pallas_call(
        body,
        out_shape=outs,
        in_specs=ins,
        out_specs=jax.tree.map(lambda _: VMEM, outs) if out_specs is None else out_specs,
        scratch_shapes=scratch,
        compiler_params=pltpu.CompilerParams(vmem_limit_bytes=limit * 2**20),
    )(*args)


def key_of(owner, flip, side):
    turned = (owner & (side - 1)) * side + owner // side
    return jnp.where(flip, turned, owner)


def sort_blocks(flip, owner_ref, slot_ref, start_ref, side):
    nb = owner_ref.shape[0]
    for k in range(side * side):
        start_ref[k] = 0
    for b in range(nb):
        key = key_of(owner_ref[b], flip, side)
        slot_ref[b] = start_ref[key]
        start_ref[key] = slot_ref[b] + 1
    total = jnp.int32(0)
    for k in range(side * side):
        held = start_ref[k]
        start_ref[k] = total
        total = total + held


def deal(parts, block_owner, side):
    nb = parts.shape[0]

    group = nb // side

    def body(owner_any_ref, parts_ref, out_ref, held_ref, owner_ref, to_ref, start_ref, in_sems, owner_sem, out_sem):
        fetches = []
        for i in range(side):
            part = pl.ds(i * group, group)
            fetches.append(pltpu.make_async_copy(parts_ref.at[part], held_ref.at[part], in_sems.at[i]))
            fetches[i].start()
        owners = pltpu.make_async_copy(owner_any_ref, owner_ref, owner_sem)
        owners.start()
        owners.wait()
        flip = lax.axis_index("c") == 1
        sort_blocks(flip, owner_ref, to_ref, start_ref, side)
        for b in range(nb):
            rank = start_ref[key_of(owner_ref[b], flip, side)] + to_ref[b]
            to_ref[b] = (rank & (side - 1)) * group + rank // side
        for i in range(side):
            fetches[i].wait()
            for b in range(i * group, (i + 1) * group):
                pltpu.make_async_copy(held_ref.at[b], out_ref.at[to_ref[b]], out_sem).start()
        pltpu.make_async_copy(held_ref, out_ref, out_sem).wait()

    scratch = [
        pltpu.VMEM(parts.shape, parts.dtype),
        pltpu.SMEM((nb,), jnp.int32),
        pltpu.SMEM((nb,), jnp.int32),
        pltpu.SMEM((side * side,), jnp.int32),
        pltpu.SemaphoreType.DMA((side,)),
        pltpu.SemaphoreType.DMA(()),
        pltpu.SemaphoreType.DMA(()),
    ]
    out = jax.ShapeDtypeStruct(parts.shape, parts.dtype)
    return local_call(body, out, [ANY, ANY], (block_owner, parts), ANY, scratch, 60)


def tables(block_owner, owner_counts, rights, side, slots):
    nb = block_owner.shape[0]

    def body(owner_ref, count_ref, right_ref, out_ref, staged_ref, slot_ref, start_ref, key_at_ref, sem):
        fetch = pltpu.make_async_copy(right_ref, staged_ref, sem)
        fetch.start()
        z, y, core = lax.axis_index("z"), lax.axis_index("y"), lax.axis_index("c")
        flip = core == 1
        u, w = jnp.where(flip, z, y), jnp.where(flip, y, z)
        sort_blocks(flip, owner_ref, slot_ref, start_ref, side)
        for b in range(nb):
            key = key_of(owner_ref[b], flip, side)
            key_at_ref[start_ref[key] + slot_ref[b]] = key

        def first(line):
            return jnp.maximum(start_ref[line * side] - u + side - 1, 0) // side

        for line in range(side):
            for s in range(slots):
                out_ref[TWO + line * slots + s] = jnp.minimum(first(line) + s, nb // side - 1)
        here = key_at_ref[jnp.minimum(first(w) * side + u, nb - 1)] & (side - 1)
        for i in range(side):
            out_ref[THREE + i] = jnp.where(here == i, 0, 1)
        for s in range(slots):
            out_ref[OWN + s] = (start_ref[w * side + u] + s) & (side - 1)
        for i in range(side):
            b = jnp.where(flip, u * side + i, i * side + u)
            key = key_of(owner_ref[b], flip, side)
            out_ref[BACK + i] = (key & (side - 1)) * slots + slot_ref[b]
        out_ref[SOURCE] = key_of(owner_ref[z * side + y], flip, side) // side
        out_ref[COUNT] = count_ref[0]
        out_ref[ROWS] = lax.axis_index("x") * 2 + core
        fetch.wait()

    scratch = [
        pltpu.SMEM((nb,), jnp.int32),
        pltpu.SMEM((side * side,), jnp.int32),
        pltpu.SMEM((nb,), jnp.int32),
        pltpu.SemaphoreType.DMA(()),
    ]
    outs = (
        jax.ShapeDtypeStruct((TABLE,), jnp.int32),
        jax.ShapeDtypeStruct(rights.shape, rights.dtype),
    )
    return local_call(
        body, outs, [SMEM, SMEM, ANY], (block_owner, owner_counts, rights), (SMEM, VMEM), scratch
    )


def sum_and_pick(got, table, base, count, sources):
    each = got.shape[0] // sources

    def body(table_ref, got_ref, out_ref, held_ref, total_ref, sems):
        def fetch(s):
            part = pl.ds(s * each, each)
            return pltpu.make_async_copy(got_ref.at[part], held_ref.at[part], sems.at[s])

        for s in range(sources):
            fetch(s).start()
        for s in range(sources):
            fetch(s).wait()
            for i in range(each):
                block = held_ref[s * each + i]
                total_ref[i] = block if s == 0 else total_ref[i] + block
        for i in range(count):
            out_ref[i] = total_ref[table_ref[base + i]]

    out = jax.ShapeDtypeStruct((count, *got.shape[1:]), got.dtype)
    scratch = [
        pltpu.VMEM(got.shape, got.dtype),
        pltpu.VMEM((each, *got.shape[1:]), got.dtype),
        pltpu.SemaphoreType.DMA((sources,)),
    ]
    return local_call(body, out, [SMEM, ANY], (table, got), None, scratch)


def sum_and_pick_here(got, table, base, count, sources):
    each = got.shape[0] // sources

    def body(table_ref, got_ref, out_ref):
        for i in range(count):
            at = table_ref[base + i]
            total = got_ref[at]
            for s in range(1, sources):
                total = total + got_ref[s * each + at]
            out_ref[i] = total

    out = jax.ShapeDtypeStruct((count, *got.shape[1:]), got.dtype)
    return local_call(body, out, [SMEM, VMEM], (table, got))


def pick_and_repeat(got, table, base, count, times):
    def body(table_ref, got_ref, out_ref):
        for i in range(count):
            block = got_ref[table_ref[base + i]]
            for t in range(times):
                out_ref[t * count + i] = block

    out = jax.ShapeDtypeStruct((times * count, *got.shape[1:]), got.dtype)
    return local_call(body, out, [SMEM, VMEM], (table, got))


def halves(a):
    high = a.astype(jnp.bfloat16)
    return high, (a - high.astype(jnp.float32)).astype(jnp.bfloat16)


def product(a, b):
    (ah, al), (bh, bl) = halves(a), halves(b)

    def dot(p, q):
        return jnp.dot(p, q, preferred_element_type=jnp.float32)

    return dot(ah, bh) + (dot(ah, bl) + dot(al, bh))


def step(whole, lefts, rights, moment, table, times):
    slots, rows, order = moment.shape

    def body(table_ref, whole_ref, left_ref, right_ref, moment_ref, moment_out_ref, send_ref, pre_ref):
        held = table_ref[COUNT]
        mine = pl.ds(pl.multiple_of(table_ref[ROWS] * rows, rows), rows)
        for s in range(slots):
            gradient = whole_ref[s]
            right_part = product(gradient, right_ref[s])
            precond = product(left_ref[s], right_part)
            pre_ref[s] = precond
            entries = order * order
            grad_mean = jnp.sum(gradient * gradient, keepdims=True) / entries
            pre_mean = jnp.sum(precond * precond, keepdims=True) / entries
            graft = jnp.sqrt(grad_mean) / jnp.sqrt(pre_mean + EPS)
            direction = graft * pre_ref[s, mine]
            before = moment_ref[s]
            fresh = BETA * before + direction
            update = BETA * fresh + direction
            moment_out_ref[s] = jnp.where(s < held, fresh, before)
            for t in range(times):
                send_ref[t * slots + s] = update

    outs = (
        jax.ShapeDtypeStruct(moment.shape, moment.dtype),
        jax.ShapeDtypeStruct((times * slots, rows, order), moment.dtype),
    )
    scratch = [pltpu.VMEM((slots, order, order), moment.dtype)]
    return local_call(
        body, outs, [SMEM, VMEM, VMEM, VMEM, VMEM], (table, whole, lefts, rights, moment), None, scratch
    )


def make(sizes):
    side = sizes[0]
    first_lines = lines(sizes, ("y", "z"))
    second_lines = lines(sizes, ("z", "y"))

    def exchange(blocks, groups):
        return lax.all_to_all(blocks, AXES, 0, 0, tiled=True, axis_index_groups=groups)

    def on_device(grads, left_root, right_root, momentum, block_owner, owner_counts):
        slots = left_root.shape[1]
        got = exchange(deal(grads[0], block_owner, side), first_lines)
        table, rights = tables(block_owner, owner_counts, right_root[0], side, slots)
        source = table[SOURCE].astype(jnp.uint32)
        lefts = lax.all_gather(left_root[0], ("x", "c"), axis=1, tiled=True)
        early = (lefts, rights, table, source)
        got, (lefts, rights, table, source) = lax.optimization_barrier((got, early))
        got = exchange(sum_and_pick(got, table, TWO, side * slots, side), second_lines)
        got = exchange(sum_and_pick_here(got, table, THREE, side, side), first_lines)
        gradient = pick_and_repeat(got, table, OWN, slots, 1)
        whole = lax.all_gather(gradient, ("x", "c"), axis=1, tiled=True)
        new_moment, send = step(whole, lefts, rights, momentum[0], table, side)
        got = exchange(send, first_lines)
        got = exchange(pick_and_repeat(got, table, BACK, side, 1), second_lines)
        zero = jnp.uint32(0)
        update = lax.dynamic_slice(got, (source, zero, zero), (1, *got.shape[1:]))
        return (update, new_moment[None])

    return on_device


def solution(mesh):
    sizes = (8, 8, 4, 2)
    fine = Mesh(mesh.devices.reshape(sizes), AXES)
    dp, rep = ("z", "y"), ("x", "c")
    in_specs = (
        P(dp, None, rep, None),
        P(dp, None, rep, None),
        P(dp, None, None, None),
        P(dp, None, rep, None),
        P(),
        P(dp),
    )
    out_specs = (P(dp, rep, None), P(dp, None, rep, None))
    return jax.shard_map(
        make(sizes), mesh=fine, in_specs=in_specs, out_specs=out_specs, check_vma=False
    )
```

```python
import jax
import jax.numpy as jnp
from jax import lax
from jax.experimental import pallas as pl
from jax.experimental.pallas import tpu as pltpu
from jax.sharding import Mesh, PartitionSpec as P

BETA = 0.9
EPS = 1e-06
AXES = ("z", "y", "x", "c")


def device(z, y, x, c, sizes):
    return ((z * sizes[1] + y) * sizes[2] + x) * sizes[3] + c


def lines(sizes, along):
    groups = []
    for x in range(sizes[2]):
        for c in range(sizes[3]):
            for fixed in range(sizes[0]):
                if along[c] == "y":
                    groups.append([device(fixed, i, x, c, sizes) for i in range(sizes[1])])
                else:
                    groups.append([device(i, fixed, x, c, sizes) for i in range(sizes[0])])
    return groups


VMEM = pl.BlockSpec(memory_space=pltpu.VMEM)
SMEM = pl.BlockSpec(memory_space=pltpu.SMEM)


ANY = pl.BlockSpec(memory_space=pl.ANY)
TWO, THREE, OWN, BACK, COUNT, ROWS, SOURCE, TABLE = 0, 16, 24, 26, 34, 35, 36, 37


def local_call(body, outs, ins, args, out_specs=None, scratch=(), limit=24):
    return pl.pallas_call(
        body,
        out_shape=outs,
        in_specs=ins,
        out_specs=jax.tree.map(lambda _: VMEM, outs) if out_specs is None else out_specs,
        scratch_shapes=scratch,
        compiler_params=pltpu.CompilerParams(vmem_limit_bytes=limit * 2**20),
    )(*args)


def key_of(owner, flip, side):
    turned = (owner & (side - 1)) * side + owner // side
    return jnp.where(flip, turned, owner)


def sort_blocks(flip, owner_ref, slot_ref, start_ref, side):
    nb = owner_ref.shape[0]
    for k in range(side * side):
        start_ref[k] = 0
    for b in range(nb):
        key = key_of(owner_ref[b], flip, side)
        slot_ref[b] = start_ref[key]
        start_ref[key] = slot_ref[b] + 1
    total = jnp.int32(0)
    for k in range(side * side):
        held = start_ref[k]
        start_ref[k] = total
        total = total + held


def deal(parts, block_owner, side):
    nb = parts.shape[0]

    group = nb // side

    def body(owner_any_ref, parts_ref, out_ref, held_ref, owner_ref, to_ref, start_ref, in_sems, owner_sem, out_sem):
        fetches = []
        for i in range(side):
            part = pl.ds(i * group, group)
            fetches.append(pltpu.make_async_copy(parts_ref.at[part], held_ref.at[part], in_sems.at[i]))
            fetches[i].start()
        owners = pltpu.make_async_copy(owner_any_ref, owner_ref, owner_sem)
        owners.start()
        owners.wait()
        flip = lax.axis_index("c") == 1
        sort_blocks(flip, owner_ref, to_ref, start_ref, side)
        for b in range(nb):
            rank = start_ref[key_of(owner_ref[b], flip, side)] + to_ref[b]
            to_ref[b] = (rank & (side - 1)) * group + rank // side
        for i in range(side):
            fetches[i].wait()
            for b in range(i * group, (i + 1) * group):
                pltpu.make_async_copy(held_ref.at[b], out_ref.at[to_ref[b]], out_sem).start()
        pltpu.make_async_copy(held_ref, out_ref, out_sem).wait()

    scratch = [
        pltpu.VMEM(parts.shape, parts.dtype),
        pltpu.SMEM((nb,), jnp.int32),
        pltpu.SMEM((nb,), jnp.int32),
        pltpu.SMEM((side * side,), jnp.int32),
        pltpu.SemaphoreType.DMA((side,)),
        pltpu.SemaphoreType.DMA(()),
        pltpu.SemaphoreType.DMA(()),
    ]
    out = jax.ShapeDtypeStruct(parts.shape, parts.dtype)
    return local_call(body, out, [ANY, ANY], (block_owner, parts), ANY, scratch, 60)


def tables(block_owner, owner_counts, rights, side, slots):
    nb = block_owner.shape[0]

    def body(owner_ref, count_ref, right_ref, out_ref, staged_ref, slot_ref, start_ref, key_at_ref, sem):
        fetch = pltpu.make_async_copy(right_ref, staged_ref, sem)
        fetch.start()
        z, y, core = lax.axis_index("z"), lax.axis_index("y"), lax.axis_index("c")
        flip = core == 1
        u, w = jnp.where(flip, z, y), jnp.where(flip, y, z)
        sort_blocks(flip, owner_ref, slot_ref, start_ref, side)
        for b in range(nb):
            key = key_of(owner_ref[b], flip, side)
            key_at_ref[start_ref[key] + slot_ref[b]] = key

        def first(line):
            return jnp.maximum(start_ref[line * side] - u + side - 1, 0) // side

        for line in range(side):
            for s in range(slots):
                out_ref[TWO + line * slots + s] = jnp.minimum(first(line) + s, nb // side - 1)
        here = key_at_ref[jnp.minimum(first(w) * side + u, nb - 1)] & (side - 1)
        for i in range(side):
            out_ref[THREE + i] = jnp.where(here == i, 0, 1)
        for s in range(slots):
            out_ref[OWN + s] = (start_ref[w * side + u] + s) & (side - 1)
        for i in range(side):
            b = jnp.where(flip, u * side + i, i * side + u)
            key = key_of(owner_ref[b], flip, side)
            out_ref[BACK + i] = (key & (side - 1)) * slots + slot_ref[b]
        out_ref[SOURCE] = key_of(owner_ref[z * side + y], flip, side) // side
        out_ref[COUNT] = count_ref[0]
        out_ref[ROWS] = lax.axis_index("x") * 2 + core
        fetch.wait()

    scratch = [
        pltpu.SMEM((nb,), jnp.int32),
        pltpu.SMEM((side * side,), jnp.int32),
        pltpu.SMEM((nb,), jnp.int32),
        pltpu.SemaphoreType.DMA(()),
    ]
    outs = (
        jax.ShapeDtypeStruct((TABLE,), jnp.int32),
        jax.ShapeDtypeStruct(rights.shape, rights.dtype),
    )
    return local_call(
        body, outs, [SMEM, SMEM, ANY], (block_owner, owner_counts, rights), (SMEM, VMEM), scratch
    )


def sum_and_pick(got, table, base, count, sources):
    each = got.shape[0] // sources

    def body(table_ref, got_ref, out_ref, held_ref, total_ref, sems):
        def fetch(s):
            part = pl.ds(s * each, each)
            return pltpu.make_async_copy(got_ref.at[part], held_ref.at[part], sems.at[s])

        for s in range(sources):
            fetch(s).start()
        for s in range(sources):
            fetch(s).wait()
            for i in range(each):
                block = held_ref[s * each + i]
                total_ref[i] = block if s == 0 else total_ref[i] + block
        for i in range(count):
            out_ref[i] = total_ref[table_ref[base + i]]

    out = jax.ShapeDtypeStruct((count, *got.shape[1:]), got.dtype)
    scratch = [
        pltpu.VMEM(got.shape, got.dtype),
        pltpu.VMEM((each, *got.shape[1:]), got.dtype),
        pltpu.SemaphoreType.DMA((sources,)),
    ]
    return local_call(body, out, [SMEM, ANY], (table, got), None, scratch)


def sum_and_pick_here(got, table, base, count, sources):
    each = got.shape[0] // sources

    def body(table_ref, got_ref, out_ref):
        for i in range(count):
            at = table_ref[base + i]
            total = got_ref[at]
            for s in range(1, sources):
                total = total + got_ref[s * each + at]
            out_ref[i] = total

    out = jax.ShapeDtypeStruct((count, *got.shape[1:]), got.dtype)
    return local_call(body, out, [SMEM, VMEM], (table, got))


def pick_and_repeat(got, table, base, count, times):
    def body(table_ref, got_ref, out_ref):
        for i in range(count):
            block = got_ref[table_ref[base + i]]
            for t in range(times):
                out_ref[t * count + i] = block

    out = jax.ShapeDtypeStruct((times * count, *got.shape[1:]), got.dtype)
    return local_call(body, out, [SMEM, VMEM], (table, got))


def product(a, b):
    return jnp.dot(a, b, precision=lax.Precision.HIGHEST, preferred_element_type=jnp.float32)


def step(whole, lefts, rights, moment, table, times):
    slots, rows, order = moment.shape

    def body(table_ref, whole_ref, left_ref, right_ref, moment_ref, moment_out_ref, send_ref, pre_ref):
        held = table_ref[COUNT]
        mine = pl.ds(pl.multiple_of(table_ref[ROWS] * rows, rows), rows)
        for s in range(slots):
            gradient = whole_ref[s]
            right_part = product(gradient, right_ref[s])
            precond = product(left_ref[s], right_part)
            pre_ref[s] = precond
            entries = order * order
            grad_mean = jnp.sum(gradient * gradient, keepdims=True) / entries
            pre_mean = jnp.sum(precond * precond, keepdims=True) / entries
            graft = jnp.sqrt(grad_mean) / jnp.sqrt(pre_mean + EPS)
            direction = graft * pre_ref[s, mine]
            before = moment_ref[s]
            fresh = BETA * before + direction
            update = BETA * fresh + direction
            moment_out_ref[s] = jnp.where(s < held, fresh, before)
            for t in range(times):
                send_ref[t * slots + s] = update

    outs = (
        jax.ShapeDtypeStruct(moment.shape, moment.dtype),
        jax.ShapeDtypeStruct((times * slots, rows, order), moment.dtype),
    )
    scratch = [pltpu.VMEM((slots, order, order), moment.dtype)]
    return local_call(
        body, outs, [SMEM, VMEM, VMEM, VMEM, VMEM], (table, whole, lefts, rights, moment), None, scratch
    )


def make(sizes):
    side = sizes[0]
    first_lines = lines(sizes, ("y", "z"))
    second_lines = lines(sizes, ("z", "y"))

    def exchange(blocks, groups):
        return lax.all_to_all(blocks, AXES, 0, 0, tiled=True, axis_index_groups=groups)

    def on_device(grads, left_root, right_root, momentum, block_owner, owner_counts):
        slots = left_root.shape[1]
        got = exchange(deal(grads[0], block_owner, side), first_lines)
        table, rights = tables(block_owner, owner_counts, right_root[0], side, slots)
        source = table[SOURCE].astype(jnp.uint32)
        lefts = lax.all_gather(left_root[0], ("x", "c"), axis=1, tiled=True)
        early = (lefts, rights, table, source)
        got, (lefts, rights, table, source) = lax.optimization_barrier((got, early))
        got = exchange(sum_and_pick(got, table, TWO, side * slots, side), second_lines)
        got = exchange(sum_and_pick_here(got, table, THREE, side, side), first_lines)
        gradient = pick_and_repeat(got, table, OWN, slots, 1)
        whole = lax.all_gather(gradient, ("x", "c"), axis=1, tiled=True)
        new_moment, send = step(whole, lefts, rights, momentum[0], table, side)
        got = exchange(send, first_lines)
        got = exchange(pick_and_repeat(got, table, BACK, side, 1), second_lines)
        zero = jnp.uint32(0)
        update = lax.dynamic_slice(got, (source, zero, zero), (1, *got.shape[1:]))
        return (update, new_moment[None])

    return on_device


def solution(mesh):
    sizes = (8, 8, 4, 2)
    fine = Mesh(mesh.devices.reshape(sizes), AXES)
    dp, rep = ("z", "y"), ("x", "c")
    in_specs = (
        P(dp, None, rep, None),
        P(dp, None, rep, None),
        P(dp, None, None, None),
        P(dp, None, rep, None),
        P(),
        P(dp),
    )
    out_specs = (P(dp, rep, None), P(dp, None, rep, None))
    return jax.shard_map(
        make(sizes), mesh=fine, in_specs=in_specs, out_specs=out_specs, check_vma=False
    )
```

```python
import jax
import jax.numpy as jnp
from jax import lax
from jax.experimental import pallas as pl
from jax.experimental.pallas import tpu as pltpu
from jax.sharding import Mesh, PartitionSpec as P

BETA = 0.9
EPS = 1e-06
AXES = ("z", "y", "x", "c")


def device(z, y, x, c, sizes):
    return ((z * sizes[1] + y) * sizes[2] + x) * sizes[3] + c


def lines(sizes, along):
    groups = []
    for x in range(sizes[2]):
        for c in range(sizes[3]):
            for fixed in range(sizes[0]):
                if along[c] == "y":
                    groups.append([device(fixed, i, x, c, sizes) for i in range(sizes[1])])
                else:
                    groups.append([device(i, fixed, x, c, sizes) for i in range(sizes[0])])
    return groups


VMEM = pl.BlockSpec(memory_space=pltpu.VMEM)
SMEM = pl.BlockSpec(memory_space=pltpu.SMEM)


ANY = pl.BlockSpec(memory_space=pl.ANY)
TWO, THREE, OWN, BACK, COUNT, ROWS, SOURCE, TABLE = 0, 16, 24, 26, 34, 35, 36, 37


def local_call(body, outs, ins, args, out_specs=None, scratch=(), limit=24):
    return pl.pallas_call(
        body,
        out_shape=outs,
        in_specs=ins,
        out_specs=jax.tree.map(lambda _: VMEM, outs) if out_specs is None else out_specs,
        scratch_shapes=scratch,
        compiler_params=pltpu.CompilerParams(vmem_limit_bytes=limit * 2**20),
    )(*args)


def key_of(owner, flip, side):
    bits = side.bit_length() - 1
    turned = ((owner & (side - 1)) << bits) | (owner >> bits)
    return jnp.where(flip, turned, owner)


def sort_blocks(flip, owner_ref, key_ref, slot_ref, start_ref, side):
    nb = owner_ref.shape[0]
    for k in range(side * side):
        start_ref[k] = 0
    for b in range(nb):
        key = key_of(owner_ref[b], flip, side)
        slot = start_ref[key]
        key_ref[b] = key
        slot_ref[b] = slot
        start_ref[key] = slot + 1
    total = jnp.int32(0)
    for k in range(side * side):
        held = start_ref[k]
        start_ref[k] = total
        total = total + held


def deal(parts, block_owner, side):
    nb = parts.shape[0]

    group = nb // side

    def body(owner_any_ref, parts_ref, out_ref, held_ref, owner_ref, key_ref, to_ref, start_ref, in_sems, owner_sem, out_sem):
        fetches = []
        for i in range(side):
            part = pl.ds(i * group, group)
            fetches.append(pltpu.make_async_copy(parts_ref.at[part], held_ref.at[part], in_sems.at[i]))
            fetches[i].start()
        owners = pltpu.make_async_copy(owner_any_ref, owner_ref, owner_sem)
        owners.start()
        owners.wait()
        flip = lax.axis_index("c") == 1
        sort_blocks(flip, owner_ref, key_ref, to_ref, start_ref, side)
        bits = side.bit_length() - 1
        for b in range(nb):
            rank = start_ref[key_ref[b]] + to_ref[b]
            to_ref[b] = (rank & (side - 1)) * group + (rank >> bits)
        for i in range(side):
            fetches[i].wait()
            for b in range(i * group, (i + 1) * group):
                pltpu.make_async_copy(held_ref.at[b], out_ref.at[to_ref[b]], out_sem).start()
        pltpu.make_async_copy(held_ref, out_ref, out_sem).wait()

    scratch = [
        pltpu.VMEM(parts.shape, parts.dtype),
        pltpu.SMEM((nb,), jnp.int32),
        pltpu.SMEM((nb,), jnp.int32),
        pltpu.SMEM((nb,), jnp.int32),
        pltpu.SMEM((side * side,), jnp.int32),
        pltpu.SemaphoreType.DMA((side,)),
        pltpu.SemaphoreType.DMA(()),
        pltpu.SemaphoreType.DMA(()),
    ]
    out = jax.ShapeDtypeStruct(parts.shape, parts.dtype)
    return local_call(body, out, [ANY, ANY], (block_owner, parts), ANY, scratch, 60)


def tables(block_owner, owner_counts, rights, side, slots):
    nb = block_owner.shape[0]

    def body(owner_ref, count_ref, right_ref, out_ref, staged_ref, key_ref, slot_ref, start_ref, key_at_ref, sem):
        fetch = pltpu.make_async_copy(right_ref, staged_ref, sem)
        fetch.start()
        z, y, core = lax.axis_index("z"), lax.axis_index("y"), lax.axis_index("c")
        flip = core == 1
        u, w = jnp.where(flip, z, y), jnp.where(flip, y, z)
        bits = side.bit_length() - 1
        sort_blocks(flip, owner_ref, key_ref, slot_ref, start_ref, side)
        for b in range(nb):
            key_at_ref[start_ref[key_ref[b]] + slot_ref[b]] = key_ref[b]

        def first(line):
            return jnp.maximum(start_ref[line * side] - u + side - 1, 0) >> bits

        for line in range(side):
            for s in range(slots):
                out_ref[TWO + line * slots + s] = jnp.minimum(first(line) + s, nb // side - 1)
        here = key_at_ref[jnp.minimum(first(w) * side + u, nb - 1)] & (side - 1)
        for i in range(side):
            out_ref[THREE + i] = jnp.where(here == i, 0, 1)
        for s in range(slots):
            out_ref[OWN + s] = (start_ref[w * side + u] + s) & (side - 1)
        for i in range(side):
            b = jnp.where(flip, u * side + i, i * side + u)
            out_ref[BACK + i] = (key_ref[b] & (side - 1)) * slots + slot_ref[b]
        out_ref[SOURCE] = key_ref[z * side + y] >> bits
        out_ref[COUNT] = count_ref[0]
        out_ref[ROWS] = lax.axis_index("x") * 2 + core
        fetch.wait()

    scratch = [
        pltpu.SMEM((nb,), jnp.int32),
        pltpu.SMEM((nb,), jnp.int32),
        pltpu.SMEM((side * side,), jnp.int32),
        pltpu.SMEM((nb,), jnp.int32),
        pltpu.SemaphoreType.DMA(()),
    ]
    outs = (
        jax.ShapeDtypeStruct((TABLE,), jnp.int32),
        jax.ShapeDtypeStruct(rights.shape, rights.dtype),
    )
    return local_call(
        body, outs, [SMEM, SMEM, ANY], (block_owner, owner_counts, rights), (SMEM, VMEM), scratch
    )


def sum_and_pick(got, table, base, count, sources):
    each = got.shape[0] // sources

    def body(table_ref, got_ref, out_ref, held_ref, total_ref, sems):
        def fetch(s):
            part = pl.ds(s * each, each)
            return pltpu.make_async_copy(got_ref.at[part], held_ref.at[part], sems.at[s])

        for s in range(sources):
            fetch(s).start()
        for s in range(sources):
            fetch(s).wait()
            for i in range(each):
                block = held_ref[s * each + i]
                total_ref[i] = block if s == 0 else total_ref[i] + block
        for i in range(count):
            out_ref[i] = total_ref[table_ref[base + i]]

    out = jax.ShapeDtypeStruct((count, *got.shape[1:]), got.dtype)
    scratch = [
        pltpu.VMEM(got.shape, got.dtype),
        pltpu.VMEM((each, *got.shape[1:]), got.dtype),
        pltpu.SemaphoreType.DMA((sources,)),
    ]
    return local_call(body, out, [SMEM, ANY], (table, got), None, scratch)


def sum_and_pick_here(got, table, base, count, sources):
    each = got.shape[0] // sources

    def body(table_ref, got_ref, out_ref):
        for i in range(count):
            at = table_ref[base + i]
            total = got_ref[at]
            for s in range(1, sources):
                total = total + got_ref[s * each + at]
            out_ref[i] = total

    out = jax.ShapeDtypeStruct((count, *got.shape[1:]), got.dtype)
    return local_call(body, out, [SMEM, VMEM], (table, got))


def pick_and_repeat(got, table, base, count, times):
    def body(table_ref, got_ref, out_ref):
        for i in range(count):
            block = got_ref[table_ref[base + i]]
            for t in range(times):
                out_ref[t * count + i] = block

    out = jax.ShapeDtypeStruct((times * count, *got.shape[1:]), got.dtype)
    return local_call(body, out, [SMEM, VMEM], (table, got))


def product(a, b):
    return jnp.dot(a, b, precision=lax.Precision.HIGHEST, preferred_element_type=jnp.float32)


def step(whole, lefts, rights, moment, table, times):
    slots, rows, order = moment.shape

    def body(table_ref, whole_ref, left_ref, right_ref, moment_ref, moment_out_ref, send_ref, pre_ref):
        held = table_ref[COUNT]
        mine = pl.ds(pl.multiple_of(table_ref[ROWS] * rows, rows), rows)
        for s in range(slots):
            gradient = whole_ref[s]
            right_part = product(gradient, right_ref[s])
            precond = product(left_ref[s], right_part)
            pre_ref[s] = precond
            entries = order * order
            grad_mean = jnp.sum(gradient * gradient, keepdims=True) / entries
            pre_mean = jnp.sum(precond * precond, keepdims=True) / entries
            graft = jnp.sqrt(grad_mean) / jnp.sqrt(pre_mean + EPS)
            direction = graft * pre_ref[s, mine]
            before = moment_ref[s]
            fresh = BETA * before + direction
            update = BETA * fresh + direction
            moment_out_ref[s] = jnp.where(s < held, fresh, before)
            for t in range(times):
                send_ref[t * slots + s] = update

    outs = (
        jax.ShapeDtypeStruct(moment.shape, moment.dtype),
        jax.ShapeDtypeStruct((times * slots, rows, order), moment.dtype),
    )
    scratch = [pltpu.VMEM((slots, order, order), moment.dtype)]
    return local_call(
        body, outs, [SMEM, VMEM, VMEM, VMEM, VMEM], (table, whole, lefts, rights, moment), None, scratch
    )


def make(sizes):
    side = sizes[0]
    first_lines = lines(sizes, ("y", "z"))
    second_lines = lines(sizes, ("z", "y"))

    def exchange(blocks, groups):
        return lax.all_to_all(blocks, AXES, 0, 0, tiled=True, axis_index_groups=groups)

    def on_device(grads, left_root, right_root, momentum, block_owner, owner_counts):
        slots = left_root.shape[1]
        got = exchange(deal(grads[0], block_owner, side), first_lines)
        table, rights = tables(block_owner, owner_counts, right_root[0], side, slots)
        source = table[SOURCE].astype(jnp.uint32)
        lefts = lax.all_gather(left_root[0], ("x", "c"), axis=1, tiled=True)
        early = (lefts, rights, table, source)
        got, (lefts, rights, table, source) = lax.optimization_barrier((got, early))
        got = exchange(sum_and_pick(got, table, TWO, side * slots, side), second_lines)
        got = exchange(sum_and_pick_here(got, table, THREE, side, side), first_lines)
        gradient = pick_and_repeat(got, table, OWN, slots, 1)
        whole = lax.all_gather(gradient, ("x", "c"), axis=1, tiled=True)
        new_moment, send = step(whole, lefts, rights, momentum[0], table, side)
        got = exchange(send, first_lines)
        got = exchange(pick_and_repeat(got, table, BACK, side, 1), second_lines)
        zero = jnp.uint32(0)
        update = lax.dynamic_slice(got, (source, zero, zero), (1, *got.shape[1:]))
        return (update, new_moment[None])

    return on_device


def solution(mesh):
    sizes = (8, 8, 4, 2)
    fine = Mesh(mesh.devices.reshape(sizes), AXES)
    dp, rep = ("z", "y"), ("x", "c")
    in_specs = (
        P(dp, None, rep, None),
        P(dp, None, rep, None),
        P(dp, None, None, None),
        P(dp, None, rep, None),
        P(),
        P(dp),
    )
    out_specs = (P(dp, rep, None), P(dp, None, rep, None))
    return jax.shard_map(
        make(sizes), mesh=fine, in_specs=in_specs, out_specs=out_specs, check_vma=False
    )
```

```python
import jax
import jax.numpy as jnp
from jax import lax
from jax.experimental import pallas as pl
from jax.experimental.pallas import tpu as pltpu
from jax.sharding import Mesh, PartitionSpec as P

BETA = 0.9
EPS = 1e-06
AXES = ("z", "y", "x", "c")


def device(z, y, x, c, sizes):
    return ((z * sizes[1] + y) * sizes[2] + x) * sizes[3] + c


def lines(sizes, along):
    groups = []
    for x in range(sizes[2]):
        for c in range(sizes[3]):
            for fixed in range(sizes[0]):
                if along[c] == "y":
                    groups.append([device(fixed, i, x, c, sizes) for i in range(sizes[1])])
                else:
                    groups.append([device(i, fixed, x, c, sizes) for i in range(sizes[0])])
    return groups


VMEM = pl.BlockSpec(memory_space=pltpu.VMEM)
SMEM = pl.BlockSpec(memory_space=pltpu.SMEM)


ANY = pl.BlockSpec(memory_space=pl.ANY)
TWO, THREE, OWN, BACK, COUNT, ROWS, SOURCE, TABLE = 0, 16, 24, 26, 34, 35, 36, 37


def local_call(body, outs, ins, args, out_specs=None, scratch=(), limit=24):
    return pl.pallas_call(
        body,
        out_shape=outs,
        in_specs=ins,
        out_specs=jax.tree.map(lambda _: VMEM, outs) if out_specs is None else out_specs,
        scratch_shapes=scratch,
        compiler_params=pltpu.CompilerParams(vmem_limit_bytes=limit * 2**20),
    )(*args)


def key_of(owner, flip, side):
    bits = side.bit_length() - 1
    turned = ((owner & (side - 1)) << bits) | (owner >> bits)
    return jnp.where(flip, turned, owner)


def sort_blocks(flip, owner_ref, key_ref, slot_ref, start_ref, side):
    nb = owner_ref.shape[0]
    for k in range(side * side):
        start_ref[k] = 0
    for b in range(nb):
        key = key_of(owner_ref[b], flip, side)
        slot = start_ref[key]
        key_ref[b] = key
        slot_ref[b] = slot
        start_ref[key] = slot + 1
    total = jnp.int32(0)
    for k in range(side * side):
        held = start_ref[k]
        start_ref[k] = total
        total = total + held


def deal(parts, block_owner, side):
    nb = parts.shape[0]

    group = nb // side

    def body(owner_any_ref, parts_ref, out_ref, held_ref, owner_ref, key_ref, to_ref, start_ref, in_sems, owner_sem, out_sem):
        fetches = []
        for i in range(side):
            part = pl.ds(i * group, group)
            fetches.append(pltpu.make_async_copy(parts_ref.at[part], held_ref.at[part], in_sems.at[i]))
            fetches[i].start()
        owners = pltpu.make_async_copy(owner_any_ref, owner_ref, owner_sem)
        owners.start()
        owners.wait()
        flip = lax.axis_index("c") == 1
        sort_blocks(flip, owner_ref, key_ref, to_ref, start_ref, side)
        bits = side.bit_length() - 1
        for b in range(nb):
            rank = start_ref[key_ref[b]] + to_ref[b]
            to_ref[b] = (rank & (side - 1)) * group + (rank >> bits)
        for i in range(side):
            fetches[i].wait()
            for b in range(i * group, (i + 1) * group):
                pltpu.make_async_copy(held_ref.at[b], out_ref.at[to_ref[b]], out_sem).start()
        pltpu.make_async_copy(held_ref, out_ref, out_sem).wait()

    scratch = [
        pltpu.VMEM(parts.shape, parts.dtype),
        pltpu.SMEM((nb,), jnp.int32),
        pltpu.SMEM((nb,), jnp.int32),
        pltpu.SMEM((nb,), jnp.int32),
        pltpu.SMEM((side * side,), jnp.int32),
        pltpu.SemaphoreType.DMA((side,)),
        pltpu.SemaphoreType.DMA(()),
        pltpu.SemaphoreType.DMA(()),
    ]
    out = jax.ShapeDtypeStruct(parts.shape, parts.dtype)
    return local_call(body, out, [ANY, ANY], (block_owner, parts), ANY, scratch, 60)


def tables(block_owner, owner_counts, rights, side, slots):
    nb = block_owner.shape[0]

    def body(owner_ref, count_ref, right_ref, out_ref, staged_ref, key_ref, slot_ref, start_ref, key_at_ref, sem):
        fetch = pltpu.make_async_copy(right_ref, staged_ref, sem)
        fetch.start()
        z, y, core = lax.axis_index("z"), lax.axis_index("y"), lax.axis_index("c")
        flip = core == 1
        u, w = jnp.where(flip, z, y), jnp.where(flip, y, z)
        bits = side.bit_length() - 1
        sort_blocks(flip, owner_ref, key_ref, slot_ref, start_ref, side)
        for b in range(nb):
            key_at_ref[start_ref[key_ref[b]] + slot_ref[b]] = key_ref[b]

        def first(line):
            return jnp.maximum(start_ref[line * side] - u + side - 1, 0) >> bits

        for line in range(side):
            for s in range(slots):
                out_ref[TWO + line * slots + s] = jnp.minimum(first(line) + s, nb // side - 1)
        here = key_at_ref[jnp.minimum(first(w) * side + u, nb - 1)] & (side - 1)
        for i in range(side):
            out_ref[THREE + i] = jnp.where(here == i, 0, 1)
        for s in range(slots):
            out_ref[OWN + s] = (start_ref[w * side + u] + s) & (side - 1)
        for i in range(side):
            b = jnp.where(flip, u * side + i, i * side + u)
            out_ref[BACK + i] = (key_ref[b] & (side - 1)) * slots + slot_ref[b]
        out_ref[SOURCE] = key_ref[z * side + y] >> bits
        out_ref[COUNT] = count_ref[0]
        out_ref[ROWS] = lax.axis_index("x") * 2 + core
        fetch.wait()

    scratch = [
        pltpu.SMEM((nb,), jnp.int32),
        pltpu.SMEM((nb,), jnp.int32),
        pltpu.SMEM((side * side,), jnp.int32),
        pltpu.SMEM((nb,), jnp.int32),
        pltpu.SemaphoreType.DMA(()),
    ]
    outs = (
        jax.ShapeDtypeStruct((TABLE,), jnp.int32),
        jax.ShapeDtypeStruct(rights.shape, rights.dtype),
    )
    return local_call(
        body, outs, [SMEM, SMEM, ANY], (block_owner, owner_counts, rights), (SMEM, VMEM), scratch
    )


def sum_and_pick(got, table, base, count, sources):
    each = got.shape[0] // sources

    def body(table_ref, got_ref, out_ref, held_ref, total_ref, sems):
        def fetch(s):
            part = pl.ds(s * each, each)
            return pltpu.make_async_copy(got_ref.at[part], held_ref.at[part], sems.at[s])

        for s in range(sources):
            fetch(s).start()
        for s in range(sources):
            fetch(s).wait()
            for i in range(each):
                block = held_ref[s * each + i]
                total_ref[i] = block if s == 0 else total_ref[i] + block
        for i in range(count):
            out_ref[i] = total_ref[table_ref[base + i]]

    out = jax.ShapeDtypeStruct((count, *got.shape[1:]), got.dtype)
    scratch = [
        pltpu.VMEM(got.shape, got.dtype),
        pltpu.VMEM((each, *got.shape[1:]), got.dtype),
        pltpu.SemaphoreType.DMA((sources,)),
    ]
    return local_call(body, out, [SMEM, ANY], (table, got), None, scratch)


def sum_and_pick_here(got, table, base, count, sources):
    each = got.shape[0] // sources

    def body(table_ref, got_ref, out_ref):
        for i in range(count):
            at = table_ref[base + i]
            total = got_ref[at]
            for s in range(1, sources):
                total = total + got_ref[s * each + at]
            out_ref[i] = total

    out = jax.ShapeDtypeStruct((count, *got.shape[1:]), got.dtype)
    return local_call(body, out, [SMEM, VMEM], (table, got))


def pick_and_repeat(got, table, base, count, times):
    def body(table_ref, got_ref, out_ref):
        for i in range(count):
            block = got_ref[table_ref[base + i]]
            for t in range(times):
                out_ref[t * count + i] = block

    out = jax.ShapeDtypeStruct((times * count, *got.shape[1:]), got.dtype)
    return local_call(body, out, [SMEM, VMEM], (table, got))


def product(a, b):
    return jnp.dot(a, b, precision=lax.Precision.HIGHEST, preferred_element_type=jnp.float32)


def right_half(own, rights):
    slots, order = rights.shape[0], rights.shape[2]
    chips, rows = own.shape[0] // slots, own.shape[1]

    def body(own_ref, right_ref, out_ref):
        for s in range(slots):
            half = jnp.concatenate([own_ref[x * slots + s] for x in range(chips)], axis=0)
            out_ref[s] = product(half, right_ref[s]).reshape(chips, rows, order)

    return pl.pallas_call(
        body,
        out_shape=jax.ShapeDtypeStruct((slots, chips, rows, order), own.dtype),
        in_specs=[VMEM, VMEM],
        out_specs=VMEM,
        cost_estimate=pl.CostEstimate(flops=2 * slots * chips * rows * order * order * 6, bytes_accessed=2**20, transcendentals=0),
        compiler_params=pltpu.CompilerParams(vmem_limit_bytes=24 * 2**20),
    )(own, rights)


def step(own, ready, other, lefts, rights, moment, table, times):
    slots, rows, order = moment.shape
    chips = own.shape[0] // slots

    def body(table_ref, own_ref, ready_ref, other_ref, left_ref, right_ref, moment_ref, moment_out_ref, send_ref, pre_ref, right_part_ref):
        held, core = table_ref[COUNT], table_ref[ROWS] & 1
        mine = pl.ds(pl.multiple_of(table_ref[ROWS] * rows, rows), rows)
        for s in range(slots):
            here = jnp.concatenate([own_ref[x * slots + s] for x in range(chips)], axis=0)
            there = jnp.concatenate([other_ref[x * slots + s] for x in range(chips)], axis=0)
            rest = product(there, right_ref[s]).reshape(chips, rows, order)
            for x in range(chips):
                right_part_ref[s, 2 * x + core] = ready_ref[s, x]
                right_part_ref[s, 2 * x + 1 - core] = rest[x]
            precond = product(left_ref[s], right_part_ref[s].reshape(order, order))
            pre_ref[s] = precond
            entries = order * order
            grad_mean = jnp.sum(here * here + there * there, keepdims=True) / entries
            pre_mean = jnp.sum(precond * precond, keepdims=True) / entries
            graft = jnp.sqrt(grad_mean) / jnp.sqrt(pre_mean + EPS)
            direction = graft * pre_ref[s, mine]
            before = moment_ref[s]
            fresh = BETA * before + direction
            update = BETA * fresh + direction
            moment_out_ref[s] = jnp.where(s < held, fresh, before)
            for t in range(times):
                send_ref[t * slots + s] = update

    outs = (
        jax.ShapeDtypeStruct(moment.shape, moment.dtype),
        jax.ShapeDtypeStruct((times * slots, rows, order), moment.dtype),
    )
    scratch = [
        pltpu.VMEM((slots, order, order), moment.dtype),
        pltpu.VMEM((slots, order // rows, rows, order), moment.dtype),
    ]
    ins = [SMEM] + [VMEM] * 6
    return local_call(body, outs, ins, (table, own, ready, other, lefts, rights, moment), None, scratch)


def make(sizes):
    side = sizes[0]
    first_lines = lines(sizes, ("y", "z"))
    second_lines = lines(sizes, ("z", "y"))

    chip_lines = [
        [device(z, y, x, c, sizes) for x in range(sizes[2])]
        for z in range(sizes[0])
        for y in range(sizes[1])
        for c in range(sizes[3])
    ]

    def exchange(blocks, groups):
        return lax.all_to_all(blocks, AXES, 0, 0, tiled=True, axis_index_groups=groups)

    def on_device(grads, left_root, right_root, momentum, block_owner, owner_counts):
        slots = left_root.shape[1]
        got = exchange(deal(grads[0], block_owner, side), first_lines)
        table, rights = tables(block_owner, owner_counts, right_root[0], side, slots)
        source = table[SOURCE].astype(jnp.uint32)
        lefts = lax.all_gather(left_root[0], ("x", "c"), axis=1, tiled=True)
        early = (lefts, rights, table, source)
        got, (lefts, rights, table, source) = lax.optimization_barrier((got, early))
        got = exchange(sum_and_pick(got, table, TWO, side * slots, side), second_lines)
        got = exchange(sum_and_pick_here(got, table, THREE, side, side), first_lines)
        own = exchange(pick_and_repeat(got, table, OWN, slots, sizes[2]), chip_lines)
        other = lax.ppermute(own, "c", [(0, 1), (1, 0)])
        ready = right_half(own, rights)
        new_moment, send = step(own, ready, other, lefts, rights, momentum[0], table, side)
        got = exchange(send, first_lines)
        got = exchange(pick_and_repeat(got, table, BACK, side, 1), second_lines)
        zero = jnp.uint32(0)
        update = lax.dynamic_slice(got, (source, zero, zero), (1, *got.shape[1:]))
        return (update, new_moment[None])

    return on_device


def solution(mesh):
    sizes = (8, 8, 4, 2)
    fine = Mesh(mesh.devices.reshape(sizes), AXES)
    dp, rep = ("z", "y"), ("x", "c")
    in_specs = (
        P(dp, None, rep, None),
        P(dp, None, rep, None),
        P(dp, None, None, None),
        P(dp, None, rep, None),
        P(),
        P(dp),
    )
    out_specs = (P(dp, rep, None), P(dp, None, rep, None))
    return jax.shard_map(
        make(sizes), mesh=fine, in_specs=in_specs, out_specs=out_specs, check_vma=False
    )
```

```python
import jax
import jax.numpy as jnp
from jax import lax
from jax.experimental import pallas as pl
from jax.experimental.pallas import tpu as pltpu
from jax.sharding import Mesh, PartitionSpec as P

BETA = 0.9
EPS = 1e-06
AXES = ("z", "y", "x", "c")


def device(z, y, x, c, sizes):
    return ((z * sizes[1] + y) * sizes[2] + x) * sizes[3] + c


def lines(sizes, along):
    groups = []
    for x in range(sizes[2]):
        for c in range(sizes[3]):
            for fixed in range(sizes[0]):
                if along[c] == "y":
                    groups.append([device(fixed, i, x, c, sizes) for i in range(sizes[1])])
                else:
                    groups.append([device(i, fixed, x, c, sizes) for i in range(sizes[0])])
    return groups


VMEM = pl.BlockSpec(memory_space=pltpu.VMEM)
SMEM = pl.BlockSpec(memory_space=pltpu.SMEM)


ANY = pl.BlockSpec(memory_space=pl.ANY)
TWO, THREE, OWN, BACK, COUNT, ROWS, SOURCE, TABLE = 0, 16, 24, 26, 34, 35, 36, 37


def local_call(body, outs, ins, args, out_specs=None, scratch=(), limit=24):
    return pl.pallas_call(
        body,
        out_shape=outs,
        in_specs=ins,
        out_specs=jax.tree.map(lambda _: VMEM, outs) if out_specs is None else out_specs,
        scratch_shapes=scratch,
        compiler_params=pltpu.CompilerParams(vmem_limit_bytes=limit * 2**20),
    )(*args)


def key_of(owner, flip, side):
    bits = side.bit_length() - 1
    turned = ((owner & (side - 1)) << bits) | (owner >> bits)
    return jnp.where(flip, turned, owner)


def sort_blocks(flip, owner_ref, key_ref, slot_ref, start_ref, side):
    nb = owner_ref.shape[0]
    for k in range(side * side):
        start_ref[k] = 0
    for b in range(nb):
        key = key_of(owner_ref[b], flip, side)
        slot = start_ref[key]
        key_ref[b] = key
        slot_ref[b] = slot
        start_ref[key] = slot + 1
    total = jnp.int32(0)
    for k in range(side * side):
        held = start_ref[k]
        start_ref[k] = total
        total = total + held


def deal(parts, block_owner, side):
    nb = parts.shape[0]

    group = nb // side

    def body(owner_any_ref, parts_ref, out_ref, held_ref, owner_ref, key_ref, to_ref, start_ref, in_sems, owner_sem, out_sem):
        fetches = []
        for i in range(side):
            part = pl.ds(i * group, group)
            fetches.append(pltpu.make_async_copy(parts_ref.at[part], held_ref.at[part], in_sems.at[i]))
            fetches[i].start()
        owners = pltpu.make_async_copy(owner_any_ref, owner_ref, owner_sem)
        owners.start()
        owners.wait()
        flip = lax.axis_index("c") == 1
        sort_blocks(flip, owner_ref, key_ref, to_ref, start_ref, side)
        bits = side.bit_length() - 1
        for b in range(nb):
            rank = start_ref[key_ref[b]] + to_ref[b]
            to_ref[b] = (rank & (side - 1)) * group + (rank >> bits)
        for i in range(side):
            fetches[i].wait()
            for b in range(i * group, (i + 1) * group):
                pltpu.make_async_copy(held_ref.at[b], out_ref.at[to_ref[b]], out_sem).start()
        pltpu.make_async_copy(held_ref, out_ref, out_sem).wait()

    scratch = [
        pltpu.VMEM(parts.shape, parts.dtype),
        pltpu.SMEM((nb,), jnp.int32),
        pltpu.SMEM((nb,), jnp.int32),
        pltpu.SMEM((nb,), jnp.int32),
        pltpu.SMEM((side * side,), jnp.int32),
        pltpu.SemaphoreType.DMA((side,)),
        pltpu.SemaphoreType.DMA(()),
        pltpu.SemaphoreType.DMA(()),
    ]
    out = jax.ShapeDtypeStruct(parts.shape, parts.dtype)
    return local_call(body, out, [ANY, ANY], (block_owner, parts), ANY, scratch, 60)


def tables(block_owner, owner_counts, rights, side, slots):
    nb = block_owner.shape[0]

    def body(owner_ref, count_ref, right_ref, out_ref, staged_ref, key_ref, slot_ref, start_ref, key_at_ref, sem):
        fetch = pltpu.make_async_copy(right_ref, staged_ref, sem)
        fetch.start()
        z, y, core = lax.axis_index("z"), lax.axis_index("y"), lax.axis_index("c")
        flip = core == 1
        u, w = jnp.where(flip, z, y), jnp.where(flip, y, z)
        bits = side.bit_length() - 1
        sort_blocks(flip, owner_ref, key_ref, slot_ref, start_ref, side)
        for b in range(nb):
            key_at_ref[start_ref[key_ref[b]] + slot_ref[b]] = key_ref[b]

        def first(line):
            return jnp.maximum(start_ref[line * side] - u + side - 1, 0) >> bits

        for line in range(side):
            for s in range(slots):
                out_ref[TWO + line * slots + s] = jnp.minimum(first(line) + s, nb // side - 1)
        here = key_at_ref[jnp.minimum(first(w) * side + u, nb - 1)] & (side - 1)
        for i in range(side):
            out_ref[THREE + i] = jnp.where(here == i, 0, 1)
        for s in range(slots):
            out_ref[OWN + s] = (start_ref[w * side + u] + s) & (side - 1)
        for i in range(side):
            b = jnp.where(flip, u * side + i, i * side + u)
            out_ref[BACK + i] = (key_ref[b] & (side - 1)) * slots + slot_ref[b]
        out_ref[SOURCE] = key_ref[z * side + y] >> bits
        out_ref[COUNT] = count_ref[0]
        out_ref[ROWS] = lax.axis_index("x") * 2 + core
        fetch.wait()

    scratch = [
        pltpu.SMEM((nb,), jnp.int32),
        pltpu.SMEM((nb,), jnp.int32),
        pltpu.SMEM((side * side,), jnp.int32),
        pltpu.SMEM((nb,), jnp.int32),
        pltpu.SemaphoreType.DMA(()),
    ]
    outs = (
        jax.ShapeDtypeStruct((TABLE,), jnp.int32),
        jax.ShapeDtypeStruct(rights.shape, rights.dtype),
    )
    return local_call(
        body, outs, [SMEM, SMEM, ANY], (block_owner, owner_counts, rights), (SMEM, VMEM), scratch
    )


def sum_and_pick(got, table, base, count, sources):
    each = got.shape[0] // sources

    def body(table_ref, got_ref, out_ref, held_ref, total_ref, sems):
        def fetch(s):
            part = pl.ds(s * each, each)
            return pltpu.make_async_copy(got_ref.at[part], held_ref.at[part], sems.at[s])

        for s in range(sources):
            fetch(s).start()
        for s in range(sources):
            fetch(s).wait()
            for i in range(each):
                block = held_ref[s * each + i]
                total_ref[i] = block if s == 0 else total_ref[i] + block
        for i in range(count):
            out_ref[i] = total_ref[table_ref[base + i]]

    out = jax.ShapeDtypeStruct((count, *got.shape[1:]), got.dtype)
    scratch = [
        pltpu.VMEM(got.shape, got.dtype),
        pltpu.VMEM((each, *got.shape[1:]), got.dtype),
        pltpu.SemaphoreType.DMA((sources,)),
    ]
    return local_call(body, out, [SMEM, ANY], (table, got), None, scratch)


def sum_and_pick_here(got, table, base, count, sources):
    each = got.shape[0] // sources

    def body(table_ref, got_ref, out_ref):
        for i in range(count):
            at = table_ref[base + i]
            total = got_ref[at]
            for s in range(1, sources):
                total = total + got_ref[s * each + at]
            out_ref[i] = total

    out = jax.ShapeDtypeStruct((count, *got.shape[1:]), got.dtype)
    return local_call(body, out, [SMEM, VMEM], (table, got))


def pick_and_repeat(got, table, base, count, times):
    def body(table_ref, got_ref, out_ref):
        for i in range(count):
            block = got_ref[table_ref[base + i]]
            for t in range(times):
                out_ref[t * count + i] = block

    out = jax.ShapeDtypeStruct((times * count, *got.shape[1:]), got.dtype)
    return local_call(body, out, [SMEM, VMEM], (table, got))


def halves(a):
    high = a.astype(jnp.bfloat16)
    return high, (a - high.astype(jnp.float32)).astype(jnp.bfloat16)


def product(a, b):
    (ah, al), (bh, bl) = halves(a), halves(b)

    def dot(p, q):
        return jnp.dot(p, q, preferred_element_type=jnp.float32)

    return dot(ah, bh) + (dot(ah, bl) + dot(al, bh))


def right_half(own, rights):
    slots, order = rights.shape[0], rights.shape[2]
    chips, rows = own.shape[0] // slots, own.shape[1]

    def body(own_ref, right_ref, out_ref):
        for s in range(slots):
            half = jnp.concatenate([own_ref[x * slots + s] for x in range(chips)], axis=0)
            out_ref[s] = product(half, right_ref[s]).reshape(chips, rows, order)

    return pl.pallas_call(
        body,
        out_shape=jax.ShapeDtypeStruct((slots, chips, rows, order), own.dtype),
        in_specs=[VMEM, VMEM],
        out_specs=VMEM,
        cost_estimate=pl.CostEstimate(flops=2 * slots * chips * rows * order * order * 6, bytes_accessed=2**20, transcendentals=0),
        compiler_params=pltpu.CompilerParams(vmem_limit_bytes=24 * 2**20),
    )(own, rights)


def step(own, ready, other, lefts, rights, moment, table, times):
    slots, rows, order = moment.shape
    chips = own.shape[0] // slots

    def body(table_ref, own_ref, ready_ref, other_ref, left_ref, right_ref, moment_ref, moment_out_ref, send_ref, pre_ref, right_part_ref):
        held, core = table_ref[COUNT], table_ref[ROWS] & 1
        mine = pl.ds(pl.multiple_of(table_ref[ROWS] * rows, rows), rows)
        for s in range(slots):
            here = jnp.concatenate([own_ref[x * slots + s] for x in range(chips)], axis=0)
            there = jnp.concatenate([other_ref[x * slots + s] for x in range(chips)], axis=0)
            rest = product(there, right_ref[s]).reshape(chips, rows, order)
            for x in range(chips):
                right_part_ref[s, 2 * x + core] = ready_ref[s, x]
                right_part_ref[s, 2 * x + 1 - core] = rest[x]
            precond = product(left_ref[s], right_part_ref[s].reshape(order, order))
            pre_ref[s] = precond
            entries = order * order
            grad_mean = jnp.sum(here * here + there * there, keepdims=True) / entries
            pre_mean = jnp.sum(precond * precond, keepdims=True) / entries
            graft = jnp.sqrt(grad_mean) / jnp.sqrt(pre_mean + EPS)
            direction = graft * pre_ref[s, mine]
            before = moment_ref[s]
            fresh = BETA * before + direction
            update = BETA * fresh + direction
            moment_out_ref[s] = jnp.where(s < held, fresh, before)
            for t in range(times):
                send_ref[t * slots + s] = update

    outs = (
        jax.ShapeDtypeStruct(moment.shape, moment.dtype),
        jax.ShapeDtypeStruct((times * slots, rows, order), moment.dtype),
    )
    scratch = [
        pltpu.VMEM((slots, order, order), moment.dtype),
        pltpu.VMEM((slots, order // rows, rows, order), moment.dtype),
    ]
    ins = [SMEM] + [VMEM] * 6
    return local_call(body, outs, ins, (table, own, ready, other, lefts, rights, moment), None, scratch)


def make(sizes):
    side = sizes[0]
    first_lines = lines(sizes, ("y", "z"))
    second_lines = lines(sizes, ("z", "y"))

    chip_lines = [
        [device(z, y, x, c, sizes) for x in range(sizes[2])]
        for z in range(sizes[0])
        for y in range(sizes[1])
        for c in range(sizes[3])
    ]

    def exchange(blocks, groups):
        return lax.all_to_all(blocks, AXES, 0, 0, tiled=True, axis_index_groups=groups)

    def on_device(grads, left_root, right_root, momentum, block_owner, owner_counts):
        slots = left_root.shape[1]
        got = exchange(deal(grads[0], block_owner, side), first_lines)
        table, rights = tables(block_owner, owner_counts, right_root[0], side, slots)
        source = table[SOURCE].astype(jnp.uint32)
        lefts = lax.all_gather(left_root[0], ("x", "c"), axis=1, tiled=True)
        early = (lefts, rights, table, source)
        got, (lefts, rights, table, source) = lax.optimization_barrier((got, early))
        got = exchange(sum_and_pick(got, table, TWO, side * slots, side), second_lines)
        got = exchange(sum_and_pick_here(got, table, THREE, side, side), first_lines)
        own = exchange(pick_and_repeat(got, table, OWN, slots, sizes[2]), chip_lines)
        other = lax.ppermute(own, "c", [(0, 1), (1, 0)])
        ready = right_half(own, rights)
        new_moment, send = step(own, ready, other, lefts, rights, momentum[0], table, side)
        got = exchange(send, first_lines)
        got = exchange(pick_and_repeat(got, table, BACK, side, 1), second_lines)
        zero = jnp.uint32(0)
        update = lax.dynamic_slice(got, (source, zero, zero), (1, *got.shape[1:]))
        return (update, new_moment[None])

    return on_device


def solution(mesh):
    sizes = (8, 8, 4, 2)
    fine = Mesh(mesh.devices.reshape(sizes), AXES)
    dp, rep = ("z", "y"), ("x", "c")
    in_specs = (
        P(dp, None, rep, None),
        P(dp, None, rep, None),
        P(dp, None, None, None),
        P(dp, None, rep, None),
        P(),
        P(dp),
    )
    out_specs = (P(dp, rep, None), P(dp, None, rep, None))
    return jax.shard_map(
        make(sizes), mesh=fine, in_specs=in_specs, out_specs=out_specs, check_vma=False
    )
```
